32 devices in a mesh: ctx: 8 (over y, x, core), grp: 4 (over z).
Axes of the slice: x: 2, y: 2, z: 4, core: 2. Of those that a mesh axis runs over, the one named last changes fastest.
Arguments:
- saved_input: bfloat16 [4, 2048, 1024], P('grp', None, 'ctx'), may hold values from -6 to 6
- out_grad: bfloat16 [4, 2048, 1024], P('grp', None, 'ctx'), may hold values from -0.1875 to 0.1875
- filters: float32 [4, 2048, 1024], P('grp', 'ctx'), may hold values from -6 to 6
- adapter_down: bfloat16 [16, 4, 2048], P(None, 'grp'), may hold values from -0.0625 to 0.0625
- adapter_up: bfloat16 [16, 4, 2048], P(None, 'grp'), may hold values from -0.25 to 0.25
Outputs:
- grad_input: bfloat16 [4, 2048, 1024], P('grp', None, 'ctx')
- grad_filter: float32 [4, 2048, 1024], P('grp', 'ctx')
- grad_down: float32 [16, 4, 2048], P(None, 'grp')
- grad_up: float32 [16, 4, 2048], P(None, 'grp')
The draws below stay inside these ranges and needn't reach their ends.
All inputs are finite; a program needn't handle non-finite values.
Results may differ from the reference program's by a relative error of at most 0.0075.
Values may be sent and summed in bfloat16 or wider, within the bound.
No kernel may reach another device: no remote copies, remote signals or barrier semaphores. Data moves between devices by JAX's collectives and lax.ppermute only.
A program may use at most 64 MiB of HBM per device.

```python
import jax
import jax.numpy as jnp
from jax import lax

D = 8192
RANK = 16
TOKENS = 1024
GROUPS = 4
GW = 2048


def shard_levels(own_key, dims, cuts, smallest, top_value):
    gain, own = 1.0, jax.random.fold_in(own_key, 6)
    for dim, blocks in cuts:
        heights = jnp.exp(jax.random.uniform(jax.random.fold_in(own, dim), (blocks,), jnp.float32, smallest / len(cuts), top_value / len(cuts)))
        gain = gain * jnp.repeat(heights, dims[dim] // blocks).reshape([-1 if axis == dim else 1 for axis in range(len(dims))])
    return gain


def centred(own_key, extent, spread, most, shards=(), kind=jnp.bfloat16):
    entries = spread * jax.random.normal(own_key, extent, jnp.float32)
    if shards:
        entries = entries * shard_levels(own_key, extent, shards, -0.22, 0.18)
    return jnp.clip(entries, -most, most).astype(kind)


def setup_inputs(seed: int = 0) -> dict:
    arg_keys = jax.random.split(jax.random.key(seed), 6)
    return {
        "saved_input": centred(arg_keys[0], (GROUPS, GW, TOKENS), 1.0, 6.0, ((0, 4), (2, 8))),
        "out_grad": centred(arg_keys[1], (GROUPS, GW, TOKENS), TOKENS ** -0.5, 0.1875, ((0, 4), (2, 8))),
        "filters": centred(arg_keys[2], (GROUPS, GW, TOKENS), 1.0, 6.0, ((0, 4), (1, 8)), jnp.float32),
        "adapter_down": centred(arg_keys[3], (RANK, GROUPS, GW), D ** -0.5, 0.0625, ((1, 4),)),
        "adapter_up": centred(arg_keys[4], (RANK, GROUPS, GW), (D // 16) ** -0.5, 0.25, ((1, 4),)),
    }


HIGH = lax.Precision.HIGHEST


def convolve_group(operands):
    adapted, gradient, kernel = operands
    points = 2 * TOKENS
    act_spec = jnp.fft.rfft(adapted.astype(jnp.float32), n=points, axis=-1)
    grad_spec = jnp.fft.rfft(gradient.astype(jnp.float32), n=points, axis=-1)
    kern_spec = jnp.fft.rfft(kernel, n=points, axis=-1)
    grad_u = jnp.fft.irfft(grad_spec * jnp.conj(kern_spec), n=points, axis=-1)[:, :TOKENS]
    grad_filt = jnp.fft.irfft(grad_spec * jnp.conj(act_spec), n=points, axis=-1)[:, :TOKENS]
    return grad_u.astype(jnp.bfloat16), grad_filt


def reference(saved_input, out_grad, filters, adapter_down, adapter_up):
    inputs = saved_input.reshape(D, TOKENS).astype(jnp.float32)
    down_map = adapter_down.reshape(RANK, D).astype(jnp.float32)
    up_map = adapter_up.reshape(RANK, D).astype(jnp.float32)
    rank_acts = jnp.einsum("rc,ct->rt", down_map, inputs, precision=HIGH)
    adapted = (inputs + jnp.einsum("rc,rt->ct", up_map, rank_acts, precision=HIGH)).astype(jnp.bfloat16)
    grad_u, grad_filter = lax.map(convolve_group, (adapted.reshape(GROUPS, GW, TOKENS), out_grad, filters))
    du_float = grad_u.reshape(D, TOKENS).astype(jnp.float32)
    rank_grad = jnp.einsum("rc,ct->rt", up_map, du_float, precision=HIGH)
    grad_input = (du_float + jnp.einsum("rc,rt->ct", down_map, rank_grad, precision=HIGH)).astype(jnp.bfloat16)
    factor = float(TOKENS) ** -0.5
    grad_down = factor * jnp.einsum("rt,ct->rc", rank_grad, inputs, precision=HIGH)
    grad_up = factor * jnp.einsum("rt,ct->rc", rank_acts, du_float, precision=HIGH)
    return (grad_input.reshape(GROUPS, GW, TOKENS), grad_filter.reshape(GROUPS, GW, TOKENS),
            grad_down.reshape(RANK, GROUPS, GW), grad_up.reshape(RANK, GROUPS, GW))
```

```python
import functools
import math

import jax
import jax.numpy as jnp
import ml_dtypes
import numpy as np
from jax import lax
from jax.experimental import pallas as pl
from jax.experimental.pallas import tpu as pltpu
from jax.sharding import PartitionSpec as P

HIGH = lax.Precision.HIGHEST
BF16 = jnp.bfloat16
F32 = jnp.float32
TABLE_ENTRIES = 1 << 22
HALF = 256
VMEM = pltpu.CompilerParams(vmem_limit_bytes=48 * 1024 * 1024)


@functools.lru_cache(maxsize=None)
def dft_table(length):
    period = 2 * length
    phase = np.outer(np.arange(length), np.arange(length)) % period * (2.0 * np.pi / period)
    cos, sin = np.cos(phase), np.sin(phase)
    sin[:, 0] = 1.0 - 2.0 * (np.arange(length) % 2)
    half = min(HALF, length)
    both = np.stack([cos.reshape(length, -1, half), sin.reshape(length, -1, half)], axis=2)
    return both.reshape(length, period).astype(ml_dtypes.bfloat16)


def dot(left, right):
    return jnp.dot(left, right, preferred_element_type=F32)


def dot_nt(left, right):
    return lax.dot_general(left, right, (((1,), (1,)), ((), ())), preferred_element_type=F32)


def dot_tn(left, right):
    return lax.dot_general(left, right, (((0,), (0,)), ((), ())), preferred_element_type=F32)


def joined(pieces):
    return jnp.concatenate([pieces[i] for i in range(pieces.shape[0])], axis=1)


def cross_spectrum(step, left, right, half, scale):
    lc, ls, rc, rs = left[:, :half], left[:, half:], right[:, :half], right[:, half:]
    first = (lax.broadcasted_iota(jnp.int32, lc.shape, 1) == 0) & (step == 0)
    cc, ss = lc * rc, ls * rs
    real = jnp.where(first, 0.5 * cc, cc + ss)
    imag = jnp.where(first, 0.5 * ss, ls * rc - lc * rs)
    return jnp.concatenate([(scale * real).astype(BF16), (scale * imag).astype(BF16)], axis=1)


def rank_acts_kernel(down_ref, tok_ref, out_ref):
    part = dot(down_ref[...], tok_ref[...]).astype(BF16)
    for i in range(out_ref.shape[0]):
        out_ref[i] = part


def filter_spec_kernel(filt_ref, table_ref, out_ref, narrow):
    @pl.when(pl.program_id(0) == 0)
    def _():
        narrow[...] = filt_ref[...].astype(BF16)

    out_ref[...] = dot(narrow[...], table_ref[...])


def grad_u_kernel(copies, grad_ref, filt_spec_ref, up_ref, table_ref, spec_ref, du_ref, rank_ref, signal, total):
    step = pl.program_id(0)
    length = table_ref.shape[0]
    half = table_ref.shape[1] // 2

    @pl.when(step == 0)
    def _():
        signal[...] = joined(grad_ref)

    spec = dot(signal[...], table_ref[...])
    spec_ref[...] = spec
    cross = cross_spectrum(step, spec, filt_spec_ref[...], half, 1.0 / length)
    part = dot_nt(cross, table_ref[...])

    @pl.when(step == 0)
    def _():
        total[...] = part

    @pl.when(step > 0)
    def _():
        total[...] += part

    @pl.when(step == pl.num_programs(0) - 1)
    def _():
        grad_u = total[...].astype(BF16)
        rank = dot(up_ref[...], grad_u).astype(BF16)
        shards, _, width = du_ref.shape
        for i in range(shards):
            du_ref[i] = grad_u[:, i * width : (i + 1) * width]
            for j in range(copies):
                rank_ref[i * copies + j] = rank[:, i * width : (i + 1) * width]


def filter_grad_kernel(
    groups, tok_ref, acts_ref, up_ref, spec_ref, du_ref, table_ref, out_ref, up_grad_ref, signal, total
):
    step = pl.program_id(0)
    length = table_ref.shape[0]
    half = table_ref.shape[1] // 2

    @pl.when(step == 0)
    def _():
        acts = []
        for i in range(tok_ref.shape[0]):
            act = acts_ref[i * groups].astype(F32)
            for j in range(1, groups):
                act = act + acts_ref[i * groups + j].astype(F32)
            acts.append(act)
        acts = jnp.concatenate(acts, axis=1).astype(BF16)
        signal[...] = (joined(tok_ref).astype(F32) + dot_tn(up_ref[...], acts)).astype(BF16)
        up_grad_ref[...] = dot_nt(acts, joined(du_ref)) * float(length) ** -0.5

    spec = dot(signal[...], table_ref[...])
    cross = cross_spectrum(step, spec_ref[...], spec, half, 1.0 / length)
    part = dot_nt(cross, table_ref[...])

    @pl.when(step == 0)
    def _():
        total[...] = part

    @pl.when(step > 0)
    def _():
        total[...] += part

    @pl.when(step == pl.num_programs(0) - 1)
    def _():
        out_ref[...] = total[...]


def rank_grad_kernel(scale, parts_ref, tok_ref, rank_ref, down_ref):
    total = parts_ref[0].astype(F32)
    for i in range(1, parts_ref.shape[0]):
        total = total + parts_ref[i].astype(F32)
    rank = total.astype(BF16)
    rank_ref[...] = rank
    down_ref[...] = (scale * dot_nt(rank, tok_ref[...])).astype(BF16)


def input_grad_kernel(du_ref, down_ref, rank_ref, out_ref):
    du = jnp.concatenate([du_ref[i] for i in range(du_ref.shape[0])], axis=0)
    out_ref[...] = (du.astype(F32) + dot_tn(down_ref[...], rank_ref[...])).astype(BF16)


def adapter_sum_kernel(down_ref, up_ref, down_out, up_out):
    total = down_ref[0].astype(F32)
    for i in range(1, down_ref.shape[0]):
        total = total + down_ref[i].astype(F32)
    down_out[:, 0, :] = total
    up_out[:, 0, :] = jnp.concatenate([up_ref[i].astype(F32) for i in range(up_ref.shape[0])], axis=1)


def shape(dims, kind):
    return jax.ShapeDtypeStruct(dims, kind)


def dense_body(mesh, saved_input, out_grad, filters, adapter_down, adapter_up):
    shards, groups = mesh.shape["ctx"], mesh.shape["grp"]
    tok_input, tok_grad, filt = saved_input[0], out_grad[0], filters[0]
    down, up = adapter_down[:, 0, :], adapter_up[:, 0, :]
    rank, width = down.shape
    tokens = tok_input.shape[1]
    chans, length = filt.shape
    table = jnp.asarray(dft_table(length))
    block = 2 * min(HALF, length)
    steps = 2 * length // block
    everyone = ("ctx", "grp")

    def swap(value, axis):
        return lax.all_to_all(value, axis, split_axis=0, concat_axis=0, tiled=True)

    whole = lambda *dims: pl.BlockSpec(dims, lambda i: (0,) * len(dims))
    table_spec = pl.BlockSpec((length, block), lambda i: (0, i))
    spec_spec = pl.BlockSpec((chans, block), lambda i: (0, i))
    work = [pltpu.VMEM((chans, length), BF16), pltpu.VMEM((chans, length), F32)]

    chan_grad = swap(tok_grad.reshape(shards, chans, tokens), "ctx")
    chan_input = swap(tok_input.reshape(shards, chans, tokens), "ctx")
    acts_parts = pl.pallas_call(
        rank_acts_kernel, out_shape=shape((shards * groups, rank, tokens), BF16), compiler_params=VMEM, name="rank_acts"
    )(down, tok_input)
    acts = swap(acts_parts, everyone)
    own_up = lax.dynamic_slice_in_dim(up, lax.axis_index("ctx") * chans, chans, axis=1)

    filt_spec = pl.pallas_call(
        filter_spec_kernel,
        out_shape=shape((chans, 2 * length), F32),
        grid=(steps,),
        in_specs=[whole(chans, length), table_spec],
        out_specs=spec_spec,
        scratch_shapes=work[:1],
        compiler_params=VMEM,
        name="filter_spec",
    )(filt, table)

    grad_spec, chan_du, rank_parts = pl.pallas_call(
        functools.partial(grad_u_kernel, groups),
        out_shape=(
            shape((chans, 2 * length), F32),
            shape((shards, chans, tokens), BF16),
            shape((shards * groups, rank, tokens), BF16),
        ),
        grid=(steps,),
        in_specs=[whole(shards, chans, tokens), spec_spec, whole(rank, chans), table_spec],
        out_specs=(spec_spec, whole(shards, chans, tokens), whole(shards * groups, rank, tokens)),
        scratch_shapes=work,
        compiler_params=VMEM,
        name="grad_u",
    )(chan_grad, filt_spec, own_up, table)

    rank_all = swap(rank_parts, everyone)
    tok_du = swap(chan_du, "ctx")

    filt_grad, up_grad = pl.pallas_call(
        functools.partial(filter_grad_kernel, groups),
        out_shape=(shape((chans, length), F32), shape((rank, chans), F32)),
        grid=(steps,),
        in_specs=[
            whole(shards, chans, tokens),
            whole(shards * groups, rank, tokens),
            whole(rank, chans),
            spec_spec,
            whole(shards, chans, tokens),
            table_spec,
        ],
        out_specs=(whole(chans, length), whole(rank, chans)),
        scratch_shapes=work,
        compiler_params=VMEM,
        name="filter_grad",
    )(chan_input, acts, own_up, grad_spec, chan_du, table)

    rank_grad, down_part = pl.pallas_call(
        functools.partial(rank_grad_kernel, float(length) ** -0.5),
        out_shape=(shape((rank, tokens), BF16), shape((rank, width), BF16)),
        compiler_params=VMEM,
        name="rank_grad",
    )(rank_all, tok_input)

    adapter_parts = jnp.concatenate([down_part, up_grad.astype(BF16)], axis=1)
    adapter_all = swap(jnp.broadcast_to(adapter_parts, (shards,) + adapter_parts.shape), "ctx")

    grad_input = pl.pallas_call(
        input_grad_kernel, out_shape=shape((width, tokens), BF16), compiler_params=VMEM, name="input_grad"
    )(tok_du, down, rank_grad)

    grad_down, grad_up = pl.pallas_call(
        adapter_sum_kernel, out_shape=(shape((rank, 1, width), F32),) * 2, compiler_params=VMEM, name="adapter_sum"
    )(adapter_all[:, :, :width], adapter_all[:, :, width:])
    return grad_input[None], filt_grad[None], grad_down, grad_up


def split_radix(points):
    radix_low = 1
    while (
        points % (radix_low * 2) == 0
        and radix_low * 2 * (radix_low * 2) <= points
        and (points // (radix_low * 2) % 2 == 0)
    ):
        radix_low = radix_low * 2
    return (radix_low, points // radix_low)


def angle_table(height, across, period):
    index_down = lax.broadcasted_iota(jnp.int32, (height, across), 0)
    index_across = lax.broadcasted_iota(jnp.int32, (height, across), 1)
    phase = (index_down * index_across % period).astype(jnp.float32) * (2.0 * math.pi / period)
    return (jnp.cos(phase), jnp.sin(phase))


def make_tables(points):
    radix_low, radix_high = split_radix(points)
    cos_one, sin_one = angle_table(radix_high, radix_high // 2, radix_high)
    first = jnp.concatenate([cos_one, -sin_one], axis=0)
    first_high = first.astype(jnp.bfloat16)
    first_low = (first - first_high.astype(jnp.float32)).astype(jnp.bfloat16)
    twist = angle_table(radix_high, radix_low, points)
    cos_two, sin_two = angle_table(radix_low, radix_low, radix_low)
    second_fwd = jnp.concatenate(
        [jnp.concatenate([cos_two, sin_two], axis=1), jnp.concatenate([-sin_two, cos_two], axis=1)],
        axis=0,
    )
    second_inv = jnp.concatenate(
        [jnp.concatenate([cos_two, -sin_two], axis=1), jnp.concatenate([sin_two, cos_two], axis=1)],
        axis=0,
    )
    last_inv = jnp.concatenate([cos_one, -sin_one], axis=0)
    return (
        radix_low,
        radix_high,
        first,
        first_high,
        first_low,
        twist,
        second_fwd,
        second_inv,
        last_inv,
    )


def forward_dft(signal, tables):
    radix_low, radix_high, first, first_high, first_low, twist, second_fwd, second_inv, last_inv = (
        tables
    )
    channels = signal.shape[0]
    blocks = signal.reshape(channels, radix_high // 2, radix_low)
    if signal.dtype == jnp.bfloat16:
        section_one = jnp.einsum(
            "kn,cnp->ckp", first_high, blocks, preferred_element_type=jnp.float32
        )
        section_one = section_one + jnp.einsum(
            "kn,cnp->ckp", first_low, blocks, preferred_element_type=jnp.float32
        )
    else:
        section_one = jnp.einsum("kn,cnp->ckp", first, blocks, precision=HIGH)
    real_one = section_one[:, :radix_high]
    imag_one = section_one[:, radix_high:]
    cos_twist, sin_twist = twist
    real_two = real_one * cos_twist + imag_one * sin_twist
    imag_two = imag_one * cos_twist - real_one * sin_twist
    joined = jnp.concatenate([real_two, imag_two], axis=2)
    spectrum = jnp.einsum("jq,ckq->cjk", second_fwd, joined, precision=HIGH)
    return (spectrum[:, :radix_low], spectrum[:, radix_low:])


def inverse_dft(spectrum, tables):
    radix_low, radix_high, first, first_high, first_low, twist, second_fwd, second_inv, last_inv = (
        tables
    )
    spec_real, spec_imag = spectrum
    channels = spec_real.shape[0]
    joined = jnp.concatenate([spec_real, spec_imag], axis=1)
    section_one = jnp.einsum("pq,cqk->cpk", second_inv, joined, precision=HIGH)
    real_one = section_one[:, :radix_low]
    imag_one = section_one[:, radix_low:]
    cos_twist = twist[0].T
    sin_twist = twist[1].T
    real_two = real_one * cos_twist - imag_one * sin_twist
    imag_two = real_one * sin_twist + imag_one * cos_twist
    stacked = jnp.concatenate([real_two, imag_two], axis=2)
    signal = jnp.einsum("kn,cpk->cnp", last_inv, stacked, precision=HIGH)
    return signal.reshape(channels, -1) / float(radix_low * radix_high)


def conj_product(spec_left, spec_right):
    left_real, left_imag = spec_left
    right_real, right_imag = spec_right
    return (
        left_real * right_real + left_imag * right_imag,
        left_imag * right_real - left_real * right_imag,
    )


def staged_body(saved_input, out_grad, filters, adapter_down, adapter_up):
    tok_input = saved_input[0]
    tok_grad = out_grad[0]
    down_rows = adapter_down[:, 0, :]
    up_float = adapter_up[:, 0, :].astype(jnp.float32)
    rank_part = jnp.dot(down_rows, tok_input, preferred_element_type=jnp.float32)
    rank_acts = lax.psum(rank_part, "grp")
    tok_act = (
        tok_input.astype(jnp.float32) + jnp.einsum("rc,rt->ct", up_float, rank_acts, precision=HIGH)
    ).astype(jnp.bfloat16)
    chan_act, chan_grad = (
        lax.all_to_all(tok_act, "ctx", split_axis=0, concat_axis=1, tiled=True),
        lax.all_to_all(tok_grad, "ctx", split_axis=0, concat_axis=1, tiled=True),
    )
    length = chan_act.shape[1]
    tables = make_tables(2 * length)
    act_spec = forward_dft(chan_act, tables)
    grad_spec = forward_dft(chan_grad, tables)
    kern_spec = forward_dft(filters[0], tables)
    chan_du = inverse_dft(conj_product(grad_spec, kern_spec), tables).astype(jnp.bfloat16)
    filt_grad = inverse_dft(conj_product(grad_spec, act_spec), tables)
    tok_du = lax.all_to_all(chan_du, "ctx", split_axis=1, concat_axis=0, tiled=True)
    du_float = tok_du.astype(jnp.float32)
    rank_grad = lax.psum(jnp.einsum("rc,ct->rt", up_float, du_float, precision=HIGH), "grp")
    grad_input = (
        du_float + jnp.einsum("rc,rt->ct", down_rows.astype(jnp.float32), rank_grad, precision=HIGH)
    ).astype(jnp.bfloat16)
    down_part = jnp.einsum("rt,ct->rc", rank_grad, tok_input.astype(jnp.float32), precision=HIGH)
    up_part = jnp.einsum("rt,ct->rc", rank_acts, du_float, precision=HIGH)
    down_sum, up_sum = lax.psum((down_part, up_part), "ctx")
    factor = float(length) ** (-0.5)
    return (
        grad_input[None],
        filt_grad[None],
        (factor * down_sum)[:, None, :],
        (factor * up_sum)[:, None, :],
    )


def body(mesh, saved_input, out_grad, filters, adapter_down, adapter_up):
    length = filters.shape[2]
    if 2 * length * length <= TABLE_ENTRIES:
        return dense_body(mesh, saved_input, out_grad, filters, adapter_down, adapter_up)
    return staged_body(saved_input, out_grad, filters, adapter_down, adapter_up)


def solution(mesh):
    placed = (
        P("grp", None, "ctx"),
        P("grp", None, "ctx"),
        P("grp", "ctx", None),
        P(None, "grp", None),
        P(None, "grp", None),
    )
    return jax.shard_map(
        functools.partial(body, mesh),
        mesh=mesh,
        in_specs=placed,
        out_specs=(
            P("grp", None, "ctx"),
            P("grp", "ctx", None),
            P(None, "grp", None),
            P(None, "grp", None),
        ),
        check_vma=False,
    )
```

```python
import functools
import math

import jax
import jax.numpy as jnp
import ml_dtypes
import numpy as np
from jax import lax
from jax.experimental import pallas as pl
from jax.experimental.pallas import tpu as pltpu
from jax.sharding import PartitionSpec as P

HIGH = lax.Precision.HIGHEST
BF16 = jnp.bfloat16
F32 = jnp.float32
TABLE_ENTRIES = 1 << 22
HALF = 256
VMEM_BYTES = 20 * 1024 * 1024


@functools.lru_cache(maxsize=None)
def dft_table(length):
    period = 2 * length
    phase = np.outer(np.arange(length), np.arange(length)) % period * (2.0 * np.pi / period)
    cos, sin = np.cos(phase), np.sin(phase)
    sin[:, 0] = 1.0 - 2.0 * (np.arange(length) % 2)
    half = min(HALF, length)
    both = np.stack([cos.reshape(length, -1, half), sin.reshape(length, -1, half)], axis=2)
    return both.reshape(length, period).astype(ml_dtypes.bfloat16)


def dot(left, right):
    return jnp.dot(left, right, preferred_element_type=F32)


def dot_nt(left, right):
    return lax.dot_general(left, right, (((1,), (1,)), ((), ())), preferred_element_type=F32)


def dot_tn(left, right):
    return lax.dot_general(left, right, (((0,), (0,)), ((), ())), preferred_element_type=F32)


def shape(dims, kind):
    return jax.ShapeDtypeStruct(dims, kind)


def own_index(index_ref, offset):
    return jnp.bitwise_xor(index_ref[0], offset)


def part(index, size):
    return pl.ds(pl.multiple_of(index * size, size), size)


def cross_spectrum(first, left, right, half, scale):
    lc, ls, rc, rs = left[:, :half], left[:, half:], right[:, :half], right[:, half:]
    cc, ss = lc * rc, ls * rs
    real, imag = cc + ss, ls * rc - lc * rs
    if first:
        lane = lax.broadcasted_iota(jnp.int32, lc.shape, 1) == 0
        real = jnp.where(lane, 0.5 * cc, real)
        imag = jnp.where(lane, 0.5 * ss, imag)
    return jnp.concatenate([(scale * real).astype(BF16), (scale * imag).astype(BF16)], axis=1)


def blocks(table_ref):
    length, period = table_ref.shape
    width = 2 * min(HALF, length)
    return [slice(i, i + width) for i in range(0, period, width)]


def filter_spec_kernel(filt_ref, table_ref, out_ref):
    out_ref[...] = dot(filt_ref[...].astype(BF16), table_ref[...])


def input_pack_kernel(index_ref, down_ref, tok_ref, sibling_ref, acts_ref, *pack_refs):
    acts_ref[...] = dot(down_ref[...], tok_ref[...]).astype(BF16)
    chans = pack_refs[0].shape[1]
    for i, pack_ref in enumerate(pack_refs):
        rows = part(own_index(index_ref, 2 * i), chans)
        pack_ref[0] = tok_ref[rows, :]
        pack_ref[1] = sibling_ref[rows, :]


def grad_u_kernel(
    copies, index_ref, grad_ref, filt_spec_ref, up_ref, acts_ref, table_ref, spec_ref, du_ref, give_ref, rank_ref, cross
):
    length = table_ref.shape[0]
    shards, chans, tokens = grad_ref.shape
    signal = jnp.concatenate([grad_ref[i] for i in range(shards)], axis=1)
    for cols in blocks(table_ref):
        half = (cols.stop - cols.start) // 2
        spec = dot(signal, table_ref[:, cols])
        spec_ref[:, cols] = spec
        cross[:, cols] = cross_spectrum(cols.start == 0, spec, filt_spec_ref[:, cols], half, 1.0 / length)
    grad_u = dot_nt(cross[...], table_ref[...]).astype(BF16)
    du_ref[...] = grad_u
    for i in range(shards // 2):
        give_ref[i] = du_ref[:, part(own_index(index_ref, 2 * i + 1), tokens)]
    rank = dot(up_ref[:, part(own_index(index_ref, 0), chans)], grad_u).astype(BF16)
    both = [jnp.concatenate([rank[:, i * tokens : (i + 1) * tokens], acts_ref[...]], axis=0) for i in range(shards)]
    for i in range(shards):
        for j in range(copies):
            rank_ref[i * copies + j] = both[i]


def du_pack_kernel(index_ref, du_ref, got_ref, *pack_refs):
    tokens = got_ref.shape[2]
    for i, pack_ref in enumerate(pack_refs):
        pack_ref[0] = du_ref[:, part(own_index(index_ref, 2 * (i + 1)), tokens)]
        pack_ref[1] = got_ref[i + 1]


def rank_kernel(groups, scale, index_ref, parts_ref, tok_ref, du_ref, rank_ref, acts_ref, adapter_ref):
    rank = rank_ref.shape[0]
    shards = parts_ref.shape[0] // groups
    width = tok_ref.shape[0]
    acts, total = [], None
    for i in range(shards):
        both = parts_ref[i * groups].astype(F32)
        for j in range(1, groups):
            both = both + parts_ref[i * groups + j].astype(F32)
        acts.append(both[rank:])
        total = both[:rank] if total is None else total + both[:rank]
    acts = jnp.concatenate(acts, axis=1).astype(BF16)
    acts_ref[...] = acts
    rank_grad = total.astype(BF16)
    rank_ref[...] = rank_grad
    adapter_ref[:, :width] = scale * dot_nt(rank_grad, tok_ref[...])
    adapter_ref[:, width:] = scale * dot_nt(acts, du_ref[...])


def chip_sum_kernel(own_ref, other_ref, out_ref):
    chans = out_ref.shape[1] - own_ref.shape[1]
    width = own_ref.shape[1] - chans
    out_ref[:, :width] = (own_ref[:, :width] + other_ref[:, :width]).astype(BF16)
    out_ref[:, width : width + chans] = own_ref[:, width:].astype(BF16)
    out_ref[:, width + chans :] = other_ref[:, width:].astype(BF16)


def filter_grad_kernel(index_ref, acts_ref, up_ref, spec_ref, table_ref, *refs):
    pack_refs, out_ref, signal, cross = refs[:-3], refs[-3], refs[-2], refs[-1]
    length = table_ref.shape[0]
    _, chans, tokens = pack_refs[0].shape
    for i, pack_ref in enumerate(pack_refs):
        for j in range(2):
            signal[:, part(own_index(index_ref, 2 * i + j), tokens)] = pack_ref[j]
    own_up = up_ref[:, part(own_index(index_ref, 0), chans)]
    act = (signal[...].astype(F32) + dot_tn(own_up, acts_ref[...])).astype(BF16)
    for cols in blocks(table_ref):
        half = (cols.stop - cols.start) // 2
        spec = dot(act, table_ref[:, cols])
        cross[:, cols] = cross_spectrum(cols.start == 0, spec_ref[:, cols], spec, half, 1.0 / length)
    out_ref[...] = dot_nt(cross[...], table_ref[...])


def input_grad_kernel(index_ref, du_ref, got_ref, down_ref, rank_ref, *refs):
    pack_refs, out_ref = refs[:-1], refs[-1]
    _, chans, tokens = got_ref.shape

    def put(offset, value):
        index = own_index(index_ref, offset)
        lift = dot_tn(down_ref[:, part(index, chans)], rank_ref[...])
        out_ref[part(index, chans), :] = (value.astype(F32) + lift).astype(BF16)

    put(0, du_ref[:, part(own_index(index_ref, 0), tokens)])
    put(1, got_ref[0])
    for i, pack_ref in enumerate(pack_refs):
        for j in range(2):
            put(2 * (i + 1) + j, pack_ref[j])


def adapter_sum_kernel(index_ref, *refs):
    part_refs, down_out, up_out, total, chunks = refs[:-4], refs[-4], refs[-3], refs[-2], refs[-1]
    width = down_out.shape[2]
    chans = (part_refs[0].shape[1] - width) // 2
    sums = [ref[:, :width].astype(F32) for ref in part_refs]
    while len(sums) > 1:
        sums = [sums[i] + sums[i + 1] for i in range(0, len(sums), 2)]
    down_out[:, 0, :] = sums[0]
    for i, ref in enumerate(part_refs):
        for j in range(2):
            block = ref[:, width + j * chans : width + (j + 1) * chans]
            chunks[:, part(own_index(index_ref, 2 * i + j), chans)] = block.astype(F32)
    up_out[:, 0, :] = chunks[...]


def dense_body(mesh, saved_input, out_grad, filters, adapter_down, adapter_up):
    shards, groups = mesh.shape["ctx"], mesh.shape["grp"]
    tok_input, tok_grad, filt = saved_input[0], out_grad[0], filters[0]
    down, up = adapter_down[:, 0, :], adapter_up[:, 0, :]
    rank, width = down.shape
    tokens = tok_input.shape[1]
    chans, length = filt.shape
    chips = shards // 2
    table = jnp.asarray(dft_table(length))
    index = lax.axis_index("ctx").reshape(1)
    scalar = pl.BlockSpec(memory_space=pltpu.SMEM)
    local = pl.BlockSpec(memory_space=pltpu.VMEM)
    product = 2 * chans * length * 2 * length

    def call(kernel, name, out_shape, args, scratch=(), flops=0, index_first=True):
        args = ((index,) if index_first else ()) + tuple(args)
        in_specs = [scalar if arg is index else local for arg in args]
        moved = sum(int(np.prod(o.shape)) * o.dtype.itemsize for o in jax.tree.leaves(out_shape))
        return pl.pallas_call(
            kernel,
            out_shape=out_shape,
            in_specs=in_specs,
            scratch_shapes=scratch,
            cost_estimate=pl.CostEstimate(flops=flops, bytes_accessed=moved, transcendentals=0),
            compiler_params=pltpu.CompilerParams(vmem_limit_bytes=VMEM_BYTES),
            name=name,
        )(*args)

    def send(value, offset):
        return lax.ppermute(value, "ctx", [(i, i ^ offset) for i in range(shards)])

    pack = shape((2, chans, tokens), BF16)
    chan_grad = lax.all_to_all(tok_grad.reshape(shards, chans, tokens), "ctx", 0, 0, tiled=True)
    sibling_input = send(tok_input, 1)
    acts_part, *input_packs = call(
        input_pack_kernel,
        "input_pack",
        (shape((rank, tokens), BF16),) + (pack,) * chips,
        (down, tok_input, sibling_input),
    )
    chan_packs = [input_packs[0]] + [send(input_packs[i], 2 * i) for i in range(1, chips)]
    filt_spec = call(
        filter_spec_kernel,
        "filter_spec",
        shape((chans, 2 * length), F32),
        (filt, table),
        flops=product,
        index_first=False,
    )
    grad_spec, chan_du, give, rank_parts = call(
        functools.partial(grad_u_kernel, groups),
        "grad_u",
        (
            shape((chans, 2 * length), F32),
            shape((chans, length), BF16),
            shape((chips, chans, tokens), BF16),
            shape((shards * groups, 2 * rank, tokens), BF16),
        ),
        (chan_grad, filt_spec, up, acts_part, table),
        scratch=[pltpu.VMEM((chans, 2 * length), BF16)],
        flops=2 * product,
    )
    rank_all = lax.all_to_all(rank_parts, ("ctx", "grp"), 0, 0, tiled=True)
    got = send(give, 1)
    du_packs = call(du_pack_kernel, "du_pack", (pack,) * (chips - 1), (chan_du, got))
    tok_packs = [send(du_packs[i], 2 * (i + 1)) for i in range(chips - 1)]

    rank_grad, acts, adapter_part = call(
        functools.partial(rank_kernel, groups, float(length) ** -0.5),
        "rank_grad",
        (shape((rank, tokens), BF16), shape((rank, length), BF16), shape((rank, width + chans), F32)),
        (rank_all, tok_input, chan_du),
    )
    chip_part = call(
        chip_sum_kernel,
        "chip_sum",
        shape((rank, width + 2 * chans), BF16),
        (adapter_part, send(adapter_part, 1)),
        index_first=False,
    )
    chip_parts = [chip_part] + [send(chip_part, 2 * i) for i in range(1, chips)]
    filt_grad = call(
        filter_grad_kernel,
        "filter_grad",
        shape((chans, length), F32),
        (acts, up, grad_spec, table, *chan_packs),
        scratch=[pltpu.VMEM((chans, length), BF16), pltpu.VMEM((chans, 2 * length), BF16)],
        flops=2 * product,
    )
    grad_input = call(
        input_grad_kernel, "input_grad", shape((width, tokens), BF16), (chan_du, got, down, rank_grad, *tok_packs)
    )
    grad_down, grad_up = call(
        adapter_sum_kernel,
        "adapter_sum",
        (shape((rank, 1, width), F32),) * 2,
        chip_parts,
        scratch=[pltpu.VMEM((rank, width), F32)] * 2,
    )
    return grad_input[None], filt_grad[None], grad_down, grad_up


def split_radix(points):
    radix_low = 1
    while (
        points % (radix_low * 2) == 0
        and radix_low * 2 * (radix_low * 2) <= points
        and (points // (radix_low * 2) % 2 == 0)
    ):
        radix_low = radix_low * 2
    return (radix_low, points // radix_low)


def angle_table(height, across, period):
    index_down = lax.broadcasted_iota(jnp.int32, (height, across), 0)
    index_across = lax.broadcasted_iota(jnp.int32, (height, across), 1)
    phase = (index_down * index_across % period).astype(jnp.float32) * (2.0 * math.pi / period)
    return (jnp.cos(phase), jnp.sin(phase))


def make_tables(points):
    radix_low, radix_high = split_radix(points)
    cos_one, sin_one = angle_table(radix_high, radix_high // 2, radix_high)
    first = jnp.concatenate([cos_one, -sin_one], axis=0)
    first_high = first.astype(jnp.bfloat16)
    first_low = (first - first_high.astype(jnp.float32)).astype(jnp.bfloat16)
    twist = angle_table(radix_high, radix_low, points)
    cos_two, sin_two = angle_table(radix_low, radix_low, radix_low)
    second_fwd = jnp.concatenate(
        [jnp.concatenate([cos_two, sin_two], axis=1), jnp.concatenate([-sin_two, cos_two], axis=1)],
        axis=0,
    )
    second_inv = jnp.concatenate(
        [jnp.concatenate([cos_two, -sin_two], axis=1), jnp.concatenate([sin_two, cos_two], axis=1)],
        axis=0,
    )
    last_inv = jnp.concatenate([cos_one, -sin_one], axis=0)
    return (
        radix_low,
        radix_high,
        first,
        first_high,
        first_low,
        twist,
        second_fwd,
        second_inv,
        last_inv,
    )


def forward_dft(signal, tables):
    radix_low, radix_high, first, first_high, first_low, twist, second_fwd, second_inv, last_inv = (
        tables
    )
    channels = signal.shape[0]
    blocks = signal.reshape(channels, radix_high // 2, radix_low)
    if signal.dtype == jnp.bfloat16:
        section_one = jnp.einsum(
            "kn,cnp->ckp", first_high, blocks, preferred_element_type=jnp.float32
        )
        section_one = section_one + jnp.einsum(
            "kn,cnp->ckp", first_low, blocks, preferred_element_type=jnp.float32
        )
    else:
        section_one = jnp.einsum("kn,cnp->ckp", first, blocks, precision=HIGH)
    real_one = section_one[:, :radix_high]
    imag_one = section_one[:, radix_high:]
    cos_twist, sin_twist = twist
    real_two = real_one * cos_twist + imag_one * sin_twist
    imag_two = imag_one * cos_twist - real_one * sin_twist
    joined = jnp.concatenate([real_two, imag_two], axis=2)
    spectrum = jnp.einsum("jq,ckq->cjk", second_fwd, joined, precision=HIGH)
    return (spectrum[:, :radix_low], spectrum[:, radix_low:])


def inverse_dft(spectrum, tables):
    radix_low, radix_high, first, first_high, first_low, twist, second_fwd, second_inv, last_inv = (
        tables
    )
    spec_real, spec_imag = spectrum
    channels = spec_real.shape[0]
    joined = jnp.concatenate([spec_real, spec_imag], axis=1)
    section_one = jnp.einsum("pq,cqk->cpk", second_inv, joined, precision=HIGH)
    real_one = section_one[:, :radix_low]
    imag_one = section_one[:, radix_low:]
    cos_twist = twist[0].T
    sin_twist = twist[1].T
    real_two = real_one * cos_twist - imag_one * sin_twist
    imag_two = real_one * sin_twist + imag_one * cos_twist
    stacked = jnp.concatenate([real_two, imag_two], axis=2)
    signal = jnp.einsum("kn,cpk->cnp", last_inv, stacked, precision=HIGH)
    return signal.reshape(channels, -1) / float(radix_low * radix_high)


def conj_product(spec_left, spec_right):
    left_real, left_imag = spec_left
    right_real, right_imag = spec_right
    return (
        left_real * right_real + left_imag * right_imag,
        left_imag * right_real - left_real * right_imag,
    )


def staged_body(saved_input, out_grad, filters, adapter_down, adapter_up):
    tok_input = saved_input[0]
    tok_grad = out_grad[0]
    down_rows = adapter_down[:, 0, :]
    up_float = adapter_up[:, 0, :].astype(jnp.float32)
    rank_part = jnp.dot(down_rows, tok_input, preferred_element_type=jnp.float32)
    rank_acts = lax.psum(rank_part, "grp")
    tok_act = (
        tok_input.astype(jnp.float32) + jnp.einsum("rc,rt->ct", up_float, rank_acts, precision=HIGH)
    ).astype(jnp.bfloat16)
    chan_act, chan_grad = (
        lax.all_to_all(tok_act, "ctx", split_axis=0, concat_axis=1, tiled=True),
        lax.all_to_all(tok_grad, "ctx", split_axis=0, concat_axis=1, tiled=True),
    )
    length = chan_act.shape[1]
    tables = make_tables(2 * length)
    act_spec = forward_dft(chan_act, tables)
    grad_spec = forward_dft(chan_grad, tables)
    kern_spec = forward_dft(filters[0], tables)
    chan_du = inverse_dft(conj_product(grad_spec, kern_spec), tables).astype(jnp.bfloat16)
    filt_grad = inverse_dft(conj_product(grad_spec, act_spec), tables)
    tok_du = lax.all_to_all(chan_du, "ctx", split_axis=1, concat_axis=0, tiled=True)
    du_float = tok_du.astype(jnp.float32)
    rank_grad = lax.psum(jnp.einsum("rc,ct->rt", up_float, du_float, precision=HIGH), "grp")
    grad_input = (
        du_float + jnp.einsum("rc,rt->ct", down_rows.astype(jnp.float32), rank_grad, precision=HIGH)
    ).astype(jnp.bfloat16)
    down_part = jnp.einsum("rt,ct->rc", rank_grad, tok_input.astype(jnp.float32), precision=HIGH)
    up_part = jnp.einsum("rt,ct->rc", rank_acts, du_float, precision=HIGH)
    down_sum, up_sum = lax.psum((down_part, up_part), "ctx")
    factor = float(length) ** (-0.5)
    return (
        grad_input[None],
        filt_grad[None],
        (factor * down_sum)[:, None, :],
        (factor * up_sum)[:, None, :],
    )


def body(mesh, saved_input, out_grad, filters, adapter_down, adapter_up):
    length = filters.shape[2]
    shards = mesh.shape["ctx"]
    if 2 * length * length <= TABLE_ENTRIES and shards > 1 and shards & (shards - 1) == 0:
        return dense_body(mesh, saved_input, out_grad, filters, adapter_down, adapter_up)
    return staged_body(saved_input, out_grad, filters, adapter_down, adapter_up)


def solution(mesh):
    placed = (
        P("grp", None, "ctx"),
        P("grp", None, "ctx"),
        P("grp", "ctx", None),
        P(None, "grp", None),
        P(None, "grp", None),
    )
    return jax.shard_map(
        functools.partial(body, mesh),
        mesh=mesh,
        in_specs=placed,
        out_specs=(
            P("grp", None, "ctx"),
            P("grp", "ctx", None),
            P(None, "grp", None),
            P(None, "grp", None),
        ),
        check_vma=False,
    )
```

```python
import functools
import math

import jax
import jax.numpy as jnp
import ml_dtypes
import numpy as np
from jax import lax
from jax.experimental import pallas as pl
from jax.experimental.pallas import tpu as pltpu
from jax.sharding import PartitionSpec as P

HIGH = lax.Precision.HIGHEST
BF16 = jnp.bfloat16
F32 = jnp.float32
TABLE_ENTRIES = 1 << 22
HALF = 256
VMEM_BYTES = 20 * 1024 * 1024


@functools.lru_cache(maxsize=None)
def dft_table(length):
    period = 2 * length
    phase = np.outer(np.arange(length), np.arange(length)) % period * (2.0 * np.pi / period)
    cos, sin = np.cos(phase), np.sin(phase)
    sin[:, 0] = 1.0 - 2.0 * (np.arange(length) % 2)
    half = min(HALF, length)
    both = np.stack([cos.reshape(length, -1, half), sin.reshape(length, -1, half)], axis=2)
    return both.reshape(length, period).astype(ml_dtypes.bfloat16)


def dot(left, right):
    return jnp.dot(left, right, preferred_element_type=F32)


def dot_nt(left, right):
    return lax.dot_general(left, right, (((1,), (1,)), ((), ())), preferred_element_type=F32)


def dot_tn(left, right):
    return lax.dot_general(left, right, (((0,), (0,)), ((), ())), preferred_element_type=F32)


def shape(dims, kind):
    return jax.ShapeDtypeStruct(dims, kind)


def own_index(index_ref, offset):
    return jnp.bitwise_xor(index_ref[0], offset)


def part(index, size):
    return pl.ds(pl.multiple_of(index * size, size), size)


def cross_spectrum(first, left, right, half, scale):
    lc, ls, rc, rs = left[:, :half], left[:, half:], right[:, :half], right[:, half:]
    cc, ss = lc * rc, ls * rs
    real, imag = cc + ss, ls * rc - lc * rs
    if first:
        lane = lax.broadcasted_iota(jnp.int32, lc.shape, 1) == 0
        real = jnp.where(lane, 0.5 * cc, real)
        imag = jnp.where(lane, 0.5 * ss, imag)
    return jnp.concatenate([(scale * real).astype(BF16), (scale * imag).astype(BF16)], axis=1)


def blocks(table_ref):
    length, period = table_ref.shape
    width = 2 * min(HALF, length)
    return [slice(i, i + width) for i in range(0, period, width)]


def filter_spec_kernel(filt_ref, table_ref, out_ref):
    out_ref[...] = dot(filt_ref[...].astype(BF16), table_ref[...])


def grad_pack_kernel(index_ref, tok_ref, sibling_ref, *pack_refs):
    chans = pack_refs[0].shape[1]
    for i, pack_ref in enumerate(pack_refs):
        rows = part(own_index(index_ref, 2 * i), chans)
        pack_ref[0] = tok_ref[rows, :]
        pack_ref[1] = sibling_ref[rows, :]


def input_pack_kernel(index_ref, down_ref, tok_ref, sibling_ref, acts_ref, *pack_refs):
    acts_ref[...] = dot(down_ref[...], tok_ref[...]).astype(BF16)
    grad_pack_kernel(index_ref, tok_ref, sibling_ref, *pack_refs)


def unpack(index_ref, pack_refs, signal):
    tokens = pack_refs[0].shape[2]
    for i, pack_ref in enumerate(pack_refs):
        for j in range(2):
            signal[:, part(own_index(index_ref, 2 * i + j), tokens)] = pack_ref[j]


def grad_u_kernel(copies, chips, index_ref, filt_spec_ref, up_ref, acts_ref, table_ref, *refs):
    pack_refs, (spec_ref, du_ref, give_ref, rank_ref, signal, cross) = refs[:chips], refs[chips:]
    length = table_ref.shape[0]
    shards = 2 * chips
    _, chans, tokens = pack_refs[0].shape
    unpack(index_ref, pack_refs, signal)
    for cols in blocks(table_ref):
        half = (cols.stop - cols.start) // 2
        spec = dot(signal[...], table_ref[:, cols])
        spec_ref[:, cols] = spec
        cross[:, cols] = cross_spectrum(cols.start == 0, spec, filt_spec_ref[:, cols], half, 1.0 / length)
    grad_u = dot_nt(cross[...], table_ref[...]).astype(BF16)
    du_ref[...] = grad_u
    for i in range(shards // 2):
        give_ref[i] = du_ref[:, part(own_index(index_ref, 2 * i + 1), tokens)]
    rank = dot(up_ref[:, part(own_index(index_ref, 0), chans)], grad_u).astype(BF16)
    both = [jnp.concatenate([rank[:, i * tokens : (i + 1) * tokens], acts_ref[...]], axis=0) for i in range(shards)]
    for i in range(shards):
        for j in range(copies):
            rank_ref[i * copies + j] = both[i]


def du_pack_kernel(index_ref, du_ref, got_ref, *pack_refs):
    tokens = got_ref.shape[2]
    for i, pack_ref in enumerate(pack_refs):
        pack_ref[0] = du_ref[:, part(own_index(index_ref, 2 * (i + 1)), tokens)]
        pack_ref[1] = got_ref[i + 1]


def rank_kernel(groups, scale, index_ref, parts_ref, tok_ref, du_ref, rank_ref, acts_ref, adapter_ref):
    rank = rank_ref.shape[0]
    shards = parts_ref.shape[0] // groups
    width = tok_ref.shape[0]
    acts, total = [], None
    for i in range(shards):
        both = parts_ref[i * groups].astype(F32)
        for j in range(1, groups):
            both = both + parts_ref[i * groups + j].astype(F32)
        acts.append(both[rank:])
        total = both[:rank] if total is None else total + both[:rank]
    acts = jnp.concatenate(acts, axis=1).astype(BF16)
    acts_ref[...] = acts
    rank_grad = total.astype(BF16)
    rank_ref[...] = rank_grad
    adapter_ref[:, :width] = scale * dot_nt(rank_grad, tok_ref[...])
    adapter_ref[:, width:] = scale * dot_nt(acts, du_ref[...])


def chip_sum_kernel(own_ref, other_ref, out_ref):
    chans = out_ref.shape[1] - own_ref.shape[1]
    width = own_ref.shape[1] - chans
    out_ref[:, :width] = (own_ref[:, :width] + other_ref[:, :width]).astype(BF16)
    out_ref[:, width : width + chans] = own_ref[:, width:].astype(BF16)
    out_ref[:, width + chans :] = other_ref[:, width:].astype(BF16)


def filter_grad_kernel(index_ref, acts_ref, up_ref, spec_ref, table_ref, *refs):
    pack_refs, out_ref, signal, cross = refs[:-3], refs[-3], refs[-2], refs[-1]
    length = table_ref.shape[0]
    _, chans, tokens = pack_refs[0].shape
    unpack(index_ref, pack_refs, signal)
    own_up = up_ref[:, part(own_index(index_ref, 0), chans)]
    act = (signal[...].astype(F32) + dot_tn(own_up, acts_ref[...])).astype(BF16)
    for cols in blocks(table_ref):
        half = (cols.stop - cols.start) // 2
        spec = dot(act, table_ref[:, cols])
        cross[:, cols] = cross_spectrum(cols.start == 0, spec_ref[:, cols], spec, half, 1.0 / length)
    out_ref[...] = dot_nt(cross[...], table_ref[...])


def input_grad_kernel(index_ref, du_ref, got_ref, down_ref, rank_ref, *refs):
    pack_refs, out_ref = refs[:-1], refs[-1]
    _, chans, tokens = got_ref.shape

    def put(offset, value):
        index = own_index(index_ref, offset)
        lift = dot_tn(down_ref[:, part(index, chans)], rank_ref[...])
        out_ref[part(index, chans), :] = (value.astype(F32) + lift).astype(BF16)

    put(0, du_ref[:, part(own_index(index_ref, 0), tokens)])
    put(1, got_ref[0])
    for i, pack_ref in enumerate(pack_refs):
        for j in range(2):
            put(2 * (i + 1) + j, pack_ref[j])


def adapter_sum_kernel(index_ref, *refs):
    part_refs, down_out, up_out, total, chunks = refs[:-4], refs[-4], refs[-3], refs[-2], refs[-1]
    width = down_out.shape[2]
    chans = (part_refs[0].shape[1] - width) // 2
    sums = [ref[:, :width].astype(F32) for ref in part_refs]
    while len(sums) > 1:
        sums = [sums[i] + sums[i + 1] for i in range(0, len(sums), 2)]
    down_out[:, 0, :] = sums[0]
    for i, ref in enumerate(part_refs):
        for j in range(2):
            block = ref[:, width + j * chans : width + (j + 1) * chans]
            chunks[:, part(own_index(index_ref, 2 * i + j), chans)] = block.astype(F32)
    up_out[:, 0, :] = chunks[...]


def dense_body(mesh, saved_input, out_grad, filters, adapter_down, adapter_up):
    shards, groups = mesh.shape["ctx"], mesh.shape["grp"]
    tok_input, tok_grad, filt = saved_input[0], out_grad[0], filters[0]
    down, up = adapter_down[:, 0, :], adapter_up[:, 0, :]
    rank, width = down.shape
    tokens = tok_input.shape[1]
    chans, length = filt.shape
    chips = shards // 2
    table = jnp.asarray(dft_table(length))
    index = lax.axis_index("ctx").reshape(1)
    scalar = pl.BlockSpec(memory_space=pltpu.SMEM)
    local = pl.BlockSpec(memory_space=pltpu.VMEM)
    product = 2 * chans * length * 2 * length

    def call(kernel, name, out_shape, args, scratch=(), flops=0, index_first=True):
        args = ((index,) if index_first else ()) + tuple(args)
        in_specs = [scalar if arg is index else local for arg in args]
        moved = sum(int(np.prod(o.shape)) * o.dtype.itemsize for o in jax.tree.leaves(out_shape))
        return pl.pallas_call(
            kernel,
            out_shape=out_shape,
            in_specs=in_specs,
            scratch_shapes=scratch,
            cost_estimate=pl.CostEstimate(flops=flops, bytes_accessed=moved, transcendentals=0),
            compiler_params=pltpu.CompilerParams(vmem_limit_bytes=VMEM_BYTES),
            name=name,
        )(*args)

    def send(value, offset):
        return lax.ppermute(value, "ctx", [(i, i ^ offset) for i in range(shards)])

    pack = shape((2, chans, tokens), BF16)
    sibling_grad = send(tok_grad, 1)
    sibling_input = send(tok_input, 1)
    grad_packs = call(grad_pack_kernel, "grad_pack", (pack,) * chips, (tok_grad, sibling_grad))
    grad_packs, tok_input = lax.optimization_barrier((grad_packs, tok_input))
    chan_grad = [grad_packs[0]] + [send(grad_packs[i], 2 * i) for i in range(1, chips)]
    acts_part, *input_packs = call(
        input_pack_kernel,
        "input_pack",
        (shape((rank, tokens), BF16),) + (pack,) * chips,
        (down, tok_input, sibling_input),
    )
    chan_packs = [input_packs[0]] + [send(input_packs[i], 2 * i) for i in range(1, chips)]
    filt_spec = call(
        filter_spec_kernel,
        "filter_spec",
        shape((chans, 2 * length), F32),
        (filt, table),
        flops=product,
        index_first=False,
    )
    grad_spec, chan_du, give, rank_parts = call(
        functools.partial(grad_u_kernel, groups, chips),
        "grad_u",
        (
            shape((chans, 2 * length), F32),
            shape((chans, length), BF16),
            shape((chips, chans, tokens), BF16),
            shape((shards * groups, 2 * rank, tokens), BF16),
        ),
        (filt_spec, up, acts_part, table, *chan_grad),
        scratch=[pltpu.VMEM((chans, length), BF16), pltpu.VMEM((chans, 2 * length), BF16)],
        flops=2 * product,
    )
    rank_parts, chan_packs = lax.optimization_barrier((rank_parts, chan_packs))
    rank_all = lax.all_to_all(rank_parts, ("ctx", "grp"), 0, 0, tiled=True)
    got = send(give, 1)
    du_packs = call(du_pack_kernel, "du_pack", (pack,) * (chips - 1), (chan_du, got))
    tok_packs = [send(du_packs[i], 2 * (i + 1)) for i in range(chips - 1)]

    rank_grad, acts, adapter_part = call(
        functools.partial(rank_kernel, groups, float(length) ** -0.5),
        "rank_grad",
        (shape((rank, tokens), BF16), shape((rank, length), BF16), shape((rank, width + chans), F32)),
        (rank_all, tok_input, chan_du),
    )
    chip_part = call(
        chip_sum_kernel,
        "chip_sum",
        shape((rank, width + 2 * chans), BF16),
        (adapter_part, send(adapter_part, 1)),
        index_first=False,
    )
    chip_parts = [chip_part] + [send(chip_part, 2 * i) for i in range(1, chips)]
    filt_grad = call(
        filter_grad_kernel,
        "filter_grad",
        shape((chans, length), F32),
        (acts, up, grad_spec, table, *chan_packs),
        scratch=[pltpu.VMEM((chans, length), BF16), pltpu.VMEM((chans, 2 * length), BF16)],
        flops=2 * product,
    )
    grad_input = call(
        input_grad_kernel, "input_grad", shape((width, tokens), BF16), (chan_du, got, down, rank_grad, *tok_packs)
    )
    grad_down, grad_up = call(
        adapter_sum_kernel,
        "adapter_sum",
        (shape((rank, 1, width), F32),) * 2,
        chip_parts,
        scratch=[pltpu.VMEM((rank, width), F32)] * 2,
    )
    return grad_input[None], filt_grad[None], grad_down, grad_up


def split_radix(points):
    radix_low = 1
    while (
        points % (radix_low * 2) == 0
        and radix_low * 2 * (radix_low * 2) <= points
        and (points // (radix_low * 2) % 2 == 0)
    ):
        radix_low = radix_low * 2
    return (radix_low, points // radix_low)


def angle_table(height, across, period):
    index_down = lax.broadcasted_iota(jnp.int32, (height, across), 0)
    index_across = lax.broadcasted_iota(jnp.int32, (height, across), 1)
    phase = (index_down * index_across % period).astype(jnp.float32) * (2.0 * math.pi / period)
    return (jnp.cos(phase), jnp.sin(phase))


def make_tables(points):
    radix_low, radix_high = split_radix(points)
    cos_one, sin_one = angle_table(radix_high, radix_high // 2, radix_high)
    first = jnp.concatenate([cos_one, -sin_one], axis=0)
    first_high = first.astype(jnp.bfloat16)
    first_low = (first - first_high.astype(jnp.float32)).astype(jnp.bfloat16)
    twist = angle_table(radix_high, radix_low, points)
    cos_two, sin_two = angle_table(radix_low, radix_low, radix_low)
    second_fwd = jnp.concatenate(
        [jnp.concatenate([cos_two, sin_two], axis=1), jnp.concatenate([-sin_two, cos_two], axis=1)],
        axis=0,
    )
    second_inv = jnp.concatenate(
        [jnp.concatenate([cos_two, -sin_two], axis=1), jnp.concatenate([sin_two, cos_two], axis=1)],
        axis=0,
    )
    last_inv = jnp.concatenate([cos_one, -sin_one], axis=0)
    return (
        radix_low,
        radix_high,
        first,
        first_high,
        first_low,
        twist,
        second_fwd,
        second_inv,
        last_inv,
    )


def forward_dft(signal, tables):
    radix_low, radix_high, first, first_high, first_low, twist, second_fwd, second_inv, last_inv = (
        tables
    )
    channels = signal.shape[0]
    blocks = signal.reshape(channels, radix_high // 2, radix_low)
    if signal.dtype == jnp.bfloat16:
        section_one = jnp.einsum(
            "kn,cnp->ckp", first_high, blocks, preferred_element_type=jnp.float32
        )
        section_one = section_one + jnp.einsum(
            "kn,cnp->ckp", first_low, blocks, preferred_element_type=jnp.float32
        )
    else:
        section_one = jnp.einsum("kn,cnp->ckp", first, blocks, precision=HIGH)
    real_one = section_one[:, :radix_high]
    imag_one = section_one[:, radix_high:]
    cos_twist, sin_twist = twist
    real_two = real_one * cos_twist + imag_one * sin_twist
    imag_two = imag_one * cos_twist - real_one * sin_twist
    joined = jnp.concatenate([real_two, imag_two], axis=2)
    spectrum = jnp.einsum("jq,ckq->cjk", second_fwd, joined, precision=HIGH)
    return (spectrum[:, :radix_low], spectrum[:, radix_low:])


def inverse_dft(spectrum, tables):
    radix_low, radix_high, first, first_high, first_low, twist, second_fwd, second_inv, last_inv = (
        tables
    )
    spec_real, spec_imag = spectrum
    channels = spec_real.shape[0]
    joined = jnp.concatenate([spec_real, spec_imag], axis=1)
    section_one = jnp.einsum("pq,cqk->cpk", second_inv, joined, precision=HIGH)
    real_one = section_one[:, :radix_low]
    imag_one = section_one[:, radix_low:]
    cos_twist = twist[0].T
    sin_twist = twist[1].T
    real_two = real_one * cos_twist - imag_one * sin_twist
    imag_two = real_one * sin_twist + imag_one * cos_twist
    stacked = jnp.concatenate([real_two, imag_two], axis=2)
    signal = jnp.einsum("kn,cpk->cnp", last_inv, stacked, precision=HIGH)
    return signal.reshape(channels, -1) / float(radix_low * radix_high)


def conj_product(spec_left, spec_right):
    left_real, left_imag = spec_left
    right_real, right_imag = spec_right
    return (
        left_real * right_real + left_imag * right_imag,
        left_imag * right_real - left_real * right_imag,
    )


def staged_body(saved_input, out_grad, filters, adapter_down, adapter_up):
    tok_input = saved_input[0]
    tok_grad = out_grad[0]
    down_rows = adapter_down[:, 0, :]
    up_float = adapter_up[:, 0, :].astype(jnp.float32)
    rank_part = jnp.dot(down_rows, tok_input, preferred_element_type=jnp.float32)
    rank_acts = lax.psum(rank_part, "grp")
    tok_act = (
        tok_input.astype(jnp.float32) + jnp.einsum("rc,rt->ct", up_float, rank_acts, precision=HIGH)
    ).astype(jnp.bfloat16)
    chan_act, chan_grad = (
        lax.all_to_all(tok_act, "ctx", split_axis=0, concat_axis=1, tiled=True),
        lax.all_to_all(tok_grad, "ctx", split_axis=0, concat_axis=1, tiled=True),
    )
    length = chan_act.shape[1]
    tables = make_tables(2 * length)
    act_spec = forward_dft(chan_act, tables)
    grad_spec = forward_dft(chan_grad, tables)
    kern_spec = forward_dft(filters[0], tables)
    chan_du = inverse_dft(conj_product(grad_spec, kern_spec), tables).astype(jnp.bfloat16)
    filt_grad = inverse_dft(conj_product(grad_spec, act_spec), tables)
    tok_du = lax.all_to_all(chan_du, "ctx", split_axis=1, concat_axis=0, tiled=True)
    du_float = tok_du.astype(jnp.float32)
    rank_grad = lax.psum(jnp.einsum("rc,ct->rt", up_float, du_float, precision=HIGH), "grp")
    grad_input = (
        du_float + jnp.einsum("rc,rt->ct", down_rows.astype(jnp.float32), rank_grad, precision=HIGH)
    ).astype(jnp.bfloat16)
    down_part = jnp.einsum("rt,ct->rc", rank_grad, tok_input.astype(jnp.float32), precision=HIGH)
    up_part = jnp.einsum("rt,ct->rc", rank_acts, du_float, precision=HIGH)
    down_sum, up_sum = lax.psum((down_part, up_part), "ctx")
    factor = float(length) ** (-0.5)
    return (
        grad_input[None],
        filt_grad[None],
        (factor * down_sum)[:, None, :],
        (factor * up_sum)[:, None, :],
    )


def body(mesh, saved_input, out_grad, filters, adapter_down, adapter_up):
    length = filters.shape[2]
    shards = mesh.shape["ctx"]
    if 2 * length * length <= TABLE_ENTRIES and shards > 1 and shards & (shards - 1) == 0:
        return dense_body(mesh, saved_input, out_grad, filters, adapter_down, adapter_up)
    return staged_body(saved_input, out_grad, filters, adapter_down, adapter_up)


def solution(mesh):
    placed = (
        P("grp", None, "ctx"),
        P("grp", None, "ctx"),
        P("grp", "ctx", None),
        P(None, "grp", None),
        P(None, "grp", None),
    )
    return jax.shard_map(
        functools.partial(body, mesh),
        mesh=mesh,
        in_specs=placed,
        out_specs=(
            P("grp", None, "ctx"),
            P("grp", "ctx", None),
            P(None, "grp", None),
            P(None, "grp", None),
        ),
        check_vma=False,
    )
```

```python
import functools
import math

import jax
import jax.numpy as jnp
import ml_dtypes
import numpy as np
from jax import lax
from jax.experimental import pallas as pl
from jax.experimental.pallas import tpu as pltpu
from jax.sharding import PartitionSpec as P

HIGH = lax.Precision.HIGHEST
BF16 = jnp.bfloat16
F32 = jnp.float32
TABLE_ENTRIES = 1 << 22
HALF = 256
VMEM_BYTES = 16 << 20


@functools.lru_cache(maxsize=None)
def dft_table(length):
    period = 2 * length
    phase = np.outer(np.arange(length), np.arange(length)) % period * (2.0 * np.pi / period)
    cos, sin = np.cos(phase), np.sin(phase)
    sin[:, 0] = 1.0 - 2.0 * (np.arange(length) % 2)
    half = min(HALF, length)
    both = np.stack([cos.reshape(length, -1, half), sin.reshape(length, -1, half)], axis=2)
    return both.reshape(length, period).astype(ml_dtypes.bfloat16)


def dot(left, right):
    return jnp.dot(left, right, preferred_element_type=F32)


def dot_nt(left, right):
    return lax.dot_general(left, right, (((1,), (1,)), ((), ())), preferred_element_type=F32)


def dot_tn(left, right):
    return lax.dot_general(left, right, (((0,), (0,)), ((), ())), preferred_element_type=F32)


def shape(dims, kind):
    return jax.ShapeDtypeStruct(dims, kind)


def own_index(offset):
    return jnp.bitwise_xor(lax.axis_index("ctx"), offset)


def part(index, size):
    return pl.ds(pl.multiple_of(index * size, size), size)


def cross_spectrum(first, left, right, half, scale):
    lc, ls, rc, rs = left[:, :half], left[:, half:], right[:, :half], right[:, half:]
    cc, ss = lc * rc, ls * rs
    real, imag = cc + ss, ls * rc - lc * rs
    if first:
        lane = lax.broadcasted_iota(jnp.int32, lc.shape, 1) == 0
        real = jnp.where(lane, 0.5 * cc, real)
        imag = jnp.where(lane, 0.5 * ss, imag)
    return jnp.concatenate([(scale * real).astype(BF16), (scale * imag).astype(BF16)], axis=1)


def blocks(table_ref):
    length, period = table_ref.shape
    width = 2 * min(HALF, length)
    return [slice(i, i + width) for i in range(0, period, width)]


def pack_kernel(tok_ref, sibling_ref, *pack_refs):
    chans = pack_refs[0].shape[1]
    for i, pack_ref in enumerate(pack_refs):
        rows = part(own_index(2 * i), chans)
        pack_ref[0] = tok_ref[rows, :]
        pack_ref[1] = sibling_ref[rows, :]


def unpack(pack_refs, signal):
    tokens = pack_refs[0].shape[2]
    for i, pack_ref in enumerate(pack_refs):
        for j in range(2):
            signal[:, part(own_index(2 * i + j), tokens)] = pack_ref[j]


def filter_spec_kernel(filt_ref, tok_ref, table_ref, down_ref, spec_ref, acts_ref):
    spec_ref[...] = dot(filt_ref[...].astype(BF16), table_ref[...])
    acts_ref[...] = dot(down_ref[...], tok_ref[...]).astype(BF16)


def grad_u_kernel(filt_spec_ref, up_ref, acts_ref, table_ref, *refs):
    pack_refs, (spec_ref, keep_ref, give_ref, signal, cross, du, rank) = refs[:-7], refs[-7:]
    length = table_ref.shape[0]
    chips = len(pack_refs)
    _, chans, tokens = pack_refs[0].shape
    ranks = up_ref.shape[0]
    unpack(pack_refs, signal)
    for cols in blocks(table_ref):
        half = (cols.stop - cols.start) // 2
        spec = dot(signal[...], table_ref[:, cols])
        spec_ref[:, cols] = spec
        cross[:, cols] = cross_spectrum(cols.start == 0, spec, filt_spec_ref[:, cols], half, 1.0 / length)
    grad_u = dot_nt(cross[...], table_ref[...]).astype(BF16)
    du[...] = grad_u
    rank[...] = dot(up_ref[:, part(own_index(0), chans)], grad_u).astype(BF16)
    low = chips * chans
    for i in range(chips):
        for j, out_ref in enumerate((keep_ref, give_ref)):
            cols = part(own_index(2 * i + j), tokens)
            out_ref[i * chans : (i + 1) * chans] = du[:, cols]
            out_ref[low + i * ranks : low + (i + 1) * ranks] = rank[:, cols]
    for out_ref in (keep_ref, give_ref):
        out_ref[low + chips * ranks :] = acts_ref[...]


def core_sum_kernel(chips, ranks, keep_ref, got_ref, out_ref):
    rows = chips * ranks
    low = keep_ref.shape[0] - rows - ranks
    total = keep_ref[low : low + rows].astype(F32) + got_ref[low : low + rows].astype(F32)
    out_ref[:rows] = total.astype(BF16)
    out_ref[rows : rows + ranks] = keep_ref[low + rows :]
    out_ref[rows + ranks :] = got_ref[low + rows :]


def pairwise(values):
    while len(values) > 1:
        values = [values[i] + values[i + 1] for i in range(0, len(values), 2)]
    return values[0]


def du_pack_kernel(groups, chans, ranks, keep_ref, got_ref, *refs):
    total = pairwise([ref[...].astype(F32) for ref in refs[:groups]]).astype(BF16)
    own_ref, pack_refs = refs[groups], refs[groups + 1 :]
    rows = (1 + len(pack_refs)) * ranks
    own_ref[:ranks] = total[:ranks]
    own_ref[ranks:] = total[rows:]
    for i, pack_ref in enumerate(pack_refs):
        block = slice((i + 1) * chans, (i + 2) * chans)
        pack_ref[:chans] = keep_ref[block]
        pack_ref[chans : 2 * chans] = got_ref[block]
        pack_ref[2 * chans : 2 * chans + ranks] = total[(i + 1) * ranks : (i + 2) * ranks]
        pack_ref[2 * chans + ranks :] = total[rows:]


def rank_kernel(scale, chans, tok_ref, keep_ref, give_ref, own_ref, *refs):
    pack_refs, (rank_ref, acts_ref, adapter_ref) = refs[:-3], refs[-3:]
    ranks, tokens = rank_ref.shape
    width = tok_ref.shape[0]
    tails = [own_ref[...]] + [ref[2 * chans :] for ref in pack_refs]
    rank_grad = pairwise([tail[:ranks].astype(F32) for tail in tails]).astype(BF16)
    rank_ref[...] = rank_grad
    adapter_ref[:, :width] = scale * dot_nt(rank_grad, tok_ref[...])
    up = None
    for i, tail in enumerate(tails):
        for j, ref in enumerate((keep_ref, give_ref)):
            act = tail[(1 + j) * ranks : (2 + j) * ranks]
            acts_ref[:, part(own_index(2 * i + j), tokens)] = act
            term = dot_nt(act, ref[i * chans : (i + 1) * chans])
            up = term if up is None else up + term
    adapter_ref[:, width:] = scale * up


def chip_sum_kernel(own_ref, other_ref, out_ref):
    chans = out_ref.shape[1] - own_ref.shape[1]
    width = own_ref.shape[1] - chans
    out_ref[:, :width] = (own_ref[:, :width] + other_ref[:, :width]).astype(BF16)
    out_ref[:, width : width + chans] = own_ref[:, width:].astype(BF16)
    out_ref[:, width + chans :] = other_ref[:, width:].astype(BF16)


def filter_grad_kernel(acts_ref, up_ref, spec_ref, table_ref, *refs):
    pack_refs, out_ref, signal, cross = refs[:-3], refs[-3], refs[-2], refs[-1]
    length = table_ref.shape[0]
    chans = pack_refs[0].shape[1]
    unpack(pack_refs, signal)
    own_up = up_ref[:, part(own_index(0), chans)]
    act = (signal[...].astype(F32) + dot_tn(own_up, acts_ref[...])).astype(BF16)
    for cols in blocks(table_ref):
        half = (cols.stop - cols.start) // 2
        spec = dot(act, table_ref[:, cols])
        cross[:, cols] = cross_spectrum(cols.start == 0, spec_ref[:, cols], spec, half, 1.0 / length)
    out_ref[...] = dot_nt(cross[...], table_ref[...])


def input_grad_kernel(keep_ref, got_ref, down_ref, rank_ref, *refs):
    pack_refs, out_ref = refs[:-1], refs[-1]
    chans = (pack_refs[0].shape[0] - 3 * rank_ref.shape[0]) // 2

    def put(offset, value):
        index = own_index(offset)
        lift = dot_tn(down_ref[:, part(index, chans)], rank_ref[...])
        out_ref[part(index, chans), :] = (value.astype(F32) + lift).astype(BF16)

    put(0, keep_ref[:chans])
    put(1, got_ref[:chans])
    for i, pack_ref in enumerate(pack_refs):
        for j in range(2):
            put(2 * (i + 1) + j, pack_ref[j * chans : (j + 1) * chans])


def adapter_sum_kernel(*refs):
    part_refs, down_out, up_out, total, chunks = refs[:-4], refs[-4], refs[-3], refs[-2], refs[-1]
    width = down_out.shape[2]
    chans = (part_refs[0].shape[1] - width) // 2
    down_out[:, 0, :] = pairwise([ref[:, :width].astype(F32) for ref in part_refs])
    for i, ref in enumerate(part_refs):
        for j in range(2):
            block = ref[:, width + j * chans : width + (j + 1) * chans]
            chunks[:, part(own_index(2 * i + j), chans)] = block.astype(F32)
    up_out[:, 0, :] = chunks[...]


def dense_body(mesh, saved_input, out_grad, filters, adapter_down, adapter_up):
    shards, groups = mesh.shape["ctx"], mesh.shape["grp"]
    tok_input, tok_grad, filt = saved_input[0], out_grad[0], filters[0]
    down, up = adapter_down[:, 0, :], adapter_up[:, 0, :]
    rank, width = down.shape
    tokens = tok_input.shape[1]
    chans, length = filt.shape
    chips = shards // 2
    table = jnp.asarray(dft_table(length))
    local = pl.BlockSpec(memory_space=pltpu.VMEM)
    product = 2 * chans * length * 2 * length

    def call(kernel, name, out_shape, args, scratch=(), flops=0):
        outs = jax.tree.leaves(out_shape)
        moved = sum(int(np.prod(o.shape)) * o.dtype.itemsize for o in outs)
        out_specs = (local,) * len(outs) if isinstance(out_shape, tuple) else local
        return pl.pallas_call(
            kernel,
            out_shape=out_shape,
            in_specs=[local] * len(args),
            out_specs=out_specs,
            scratch_shapes=scratch,
            cost_estimate=pl.CostEstimate(flops=flops, bytes_accessed=moved, transcendentals=0),
            compiler_params=pltpu.CompilerParams(vmem_limit_bytes=VMEM_BYTES),
            name=name,
        )(*args)

    def send(value, offset, axis="ctx"):
        return lax.ppermute(value, axis, [(i, i ^ offset) for i in range(mesh.shape[axis])])

    def packed(own, sibling, name):
        return call(pack_kernel, name, (pack,) * chips, (own, sibling))

    def to_chips(packs):
        return [packs[0]] + [send(packs[i], 2 * i) for i in range(1, chips)]

    vmem = pltpu.VMEM
    pack = shape((2, chans, tokens), BF16)
    sibling_grad = send(tok_grad, 1)
    sibling_input = send(tok_input, 1)
    grad_packs = packed(tok_grad, sibling_grad, "grad_pack")
    grad_packs, filt, tok_input = lax.optimization_barrier((grad_packs, filt, tok_input))
    chan_grad = to_chips(grad_packs)
    filt_spec, acts_part = call(
        filter_spec_kernel,
        "filter_spec",
        (shape((chans, 2 * length), F32), shape((rank, tokens), BF16)),
        (filt, tok_input, table, down),
        flops=product,
    )
    input_packs = packed(tok_input, sibling_input, "input_pack")
    half_du = shape((chips * (chans + rank) + rank, tokens), BF16)
    grad_spec, keep, give = call(
        grad_u_kernel,
        "grad_u",
        (shape((chans, 2 * length), F32), half_du, half_du),
        (filt_spec, up, acts_part, table, *chan_grad),
        scratch=[
            vmem((chans, length), BF16),
            vmem((chans, 2 * length), BF16),
            vmem((chans, length), BF16),
            vmem((rank, length), BF16),
        ],
        flops=2 * product,
    )
    got = send(give, 1)
    input_packs, got = lax.optimization_barrier((input_packs, got))
    core_part = call(
        functools.partial(core_sum_kernel, chips, rank),
        "core_sum",
        shape(((chips + 2) * rank, tokens), BF16),
        (keep, got),
    )
    chan_packs = to_chips(input_packs)
    core_parts = [core_part] + [send(core_part, i, "grp") for i in range(1, groups)]
    own_tail, *du_packs = call(
        functools.partial(du_pack_kernel, groups, chans, rank),
        "du_pack",
        (shape((3 * rank, tokens), BF16),) + (shape((2 * chans + 3 * rank, tokens), BF16),) * (chips - 1),
        (keep, got, *core_parts),
    )
    tok_packs = [send(du_packs[i], 2 * (i + 1)) for i in range(chips - 1)]
    rank_grad, acts, adapter_part = call(
        functools.partial(rank_kernel, float(length) ** -0.5, chans),
        "rank_grad",
        (shape((rank, tokens), BF16), shape((rank, length), BF16), shape((rank, width + chans), F32)),
        (tok_input, keep, give, own_tail, *tok_packs),
    )
    chip_part = call(
        chip_sum_kernel,
        "chip_sum",
        shape((rank, width + 2 * chans), BF16),
        (adapter_part, send(adapter_part, 1)),
    )
    chip_parts = [chip_part] + [send(chip_part, 2 * i) for i in range(1, chips)]
    filt_grad = call(
        filter_grad_kernel,
        "filter_grad",
        shape((chans, length), F32),
        (acts, up, grad_spec, table, *chan_packs),
        scratch=[vmem((chans, length), BF16), vmem((chans, 2 * length), BF16)],
        flops=2 * product,
    )
    grad_input = call(
        input_grad_kernel, "input_grad", shape((width, tokens), BF16), (keep, got, down, rank_grad, *tok_packs)
    )
    grad_down, grad_up = call(
        adapter_sum_kernel,
        "adapter_sum",
        (shape((rank, 1, width), F32),) * 2,
        chip_parts,
        scratch=[pltpu.VMEM((rank, width), F32)] * 2,
    )
    return grad_input[None], filt_grad[None], grad_down, grad_up


def split_radix(points):
    radix_low = 1
    while (
        points % (radix_low * 2) == 0
        and radix_low * 2 * (radix_low * 2) <= points
        and (points // (radix_low * 2) % 2 == 0)
    ):
        radix_low = radix_low * 2
    return (radix_low, points // radix_low)


def angle_table(height, across, period):
    index_down = lax.broadcasted_iota(jnp.int32, (height, across), 0)
    index_across = lax.broadcasted_iota(jnp.int32, (height, across), 1)
    phase = (index_down * index_across % period).astype(jnp.float32) * (2.0 * math.pi / period)
    return (jnp.cos(phase), jnp.sin(phase))


def make_tables(points):
    radix_low, radix_high = split_radix(points)
    cos_one, sin_one = angle_table(radix_high, radix_high // 2, radix_high)
    first = jnp.concatenate([cos_one, -sin_one], axis=0)
    first_high = first.astype(jnp.bfloat16)
    first_low = (first - first_high.astype(jnp.float32)).astype(jnp.bfloat16)
    twist = angle_table(radix_high, radix_low, points)
    cos_two, sin_two = angle_table(radix_low, radix_low, radix_low)
    second_fwd = jnp.concatenate(
        [jnp.concatenate([cos_two, sin_two], axis=1), jnp.concatenate([-sin_two, cos_two], axis=1)],
        axis=0,
    )
    second_inv = jnp.concatenate(
        [jnp.concatenate([cos_two, -sin_two], axis=1), jnp.concatenate([sin_two, cos_two], axis=1)],
        axis=0,
    )
    last_inv = jnp.concatenate([cos_one, -sin_one], axis=0)
    return (
        radix_low,
        radix_high,
        first,
        first_high,
        first_low,
        twist,
        second_fwd,
        second_inv,
        last_inv,
    )


def forward_dft(signal, tables):
    radix_low, radix_high, first, first_high, first_low, twist, second_fwd, second_inv, last_inv = (
        tables
    )
    channels = signal.shape[0]
    blocks = signal.reshape(channels, radix_high // 2, radix_low)
    if signal.dtype == jnp.bfloat16:
        section_one = jnp.einsum(
            "kn,cnp->ckp", first_high, blocks, preferred_element_type=jnp.float32
        )
        section_one = section_one + jnp.einsum(
            "kn,cnp->ckp", first_low, blocks, preferred_element_type=jnp.float32
        )
    else:
        section_one = jnp.einsum("kn,cnp->ckp", first, blocks, precision=HIGH)
    real_one = section_one[:, :radix_high]
    imag_one = section_one[:, radix_high:]
    cos_twist, sin_twist = twist
    real_two = real_one * cos_twist + imag_one * sin_twist
    imag_two = imag_one * cos_twist - real_one * sin_twist
    joined = jnp.concatenate([real_two, imag_two], axis=2)
    spectrum = jnp.einsum("jq,ckq->cjk", second_fwd, joined, precision=HIGH)
    return (spectrum[:, :radix_low], spectrum[:, radix_low:])


def inverse_dft(spectrum, tables):
    radix_low, radix_high, first, first_high, first_low, twist, second_fwd, second_inv, last_inv = (
        tables
    )
    spec_real, spec_imag = spectrum
    channels = spec_real.shape[0]
    joined = jnp.concatenate([spec_real, spec_imag], axis=1)
    section_one = jnp.einsum("pq,cqk->cpk", second_inv, joined, precision=HIGH)
    real_one = section_one[:, :radix_low]
    imag_one = section_one[:, radix_low:]
    cos_twist = twist[0].T
    sin_twist = twist[1].T
    real_two = real_one * cos_twist - imag_one * sin_twist
    imag_two = real_one * sin_twist + imag_one * cos_twist
    stacked = jnp.concatenate([real_two, imag_two], axis=2)
    signal = jnp.einsum("kn,cpk->cnp", last_inv, stacked, precision=HIGH)
    return signal.reshape(channels, -1) / float(radix_low * radix_high)


def conj_product(spec_left, spec_right):
    left_real, left_imag = spec_left
    right_real, right_imag = spec_right
    return (
        left_real * right_real + left_imag * right_imag,
        left_imag * right_real - left_real * right_imag,
    )


def staged_body(saved_input, out_grad, filters, adapter_down, adapter_up):
    tok_input = saved_input[0]
    tok_grad = out_grad[0]
    down_rows = adapter_down[:, 0, :]
    up_float = adapter_up[:, 0, :].astype(jnp.float32)
    rank_part = jnp.dot(down_rows, tok_input, preferred_element_type=jnp.float32)
    rank_acts = lax.psum(rank_part, "grp")
    tok_act = (
        tok_input.astype(jnp.float32) + jnp.einsum("rc,rt->ct", up_float, rank_acts, precision=HIGH)
    ).astype(jnp.bfloat16)
    chan_act, chan_grad = (
        lax.all_to_all(tok_act, "ctx", split_axis=0, concat_axis=1, tiled=True),
        lax.all_to_all(tok_grad, "ctx", split_axis=0, concat_axis=1, tiled=True),
    )
    length = chan_act.shape[1]
    tables = make_tables(2 * length)
    act_spec = forward_dft(chan_act, tables)
    grad_spec = forward_dft(chan_grad, tables)
    kern_spec = forward_dft(filters[0], tables)
    chan_du = inverse_dft(conj_product(grad_spec, kern_spec), tables).astype(jnp.bfloat16)
    filt_grad = inverse_dft(conj_product(grad_spec, act_spec), tables)
    tok_du = lax.all_to_all(chan_du, "ctx", split_axis=1, concat_axis=0, tiled=True)
    du_float = tok_du.astype(jnp.float32)
    rank_grad = lax.psum(jnp.einsum("rc,ct->rt", up_float, du_float, precision=HIGH), "grp")
    grad_input = (
        du_float + jnp.einsum("rc,rt->ct", down_rows.astype(jnp.float32), rank_grad, precision=HIGH)
    ).astype(jnp.bfloat16)
    down_part = jnp.einsum("rt,ct->rc", rank_grad, tok_input.astype(jnp.float32), precision=HIGH)
    up_part = jnp.einsum("rt,ct->rc", rank_acts, du_float, precision=HIGH)
    down_sum, up_sum = lax.psum((down_part, up_part), "ctx")
    factor = float(length) ** (-0.5)
    return (
        grad_input[None],
        filt_grad[None],
        (factor * down_sum)[:, None, :],
        (factor * up_sum)[:, None, :],
    )


def body(mesh, saved_input, out_grad, filters, adapter_down, adapter_up):
    length = filters.shape[2]
    shards, groups = mesh.shape["ctx"], mesh.shape["grp"]
    paired = shards > 1 and shards & (shards - 1) == 0 and groups & (groups - 1) == 0
    if 2 * length * length <= TABLE_ENTRIES and paired:
        return dense_body(mesh, saved_input, out_grad, filters, adapter_down, adapter_up)
    return staged_body(saved_input, out_grad, filters, adapter_down, adapter_up)


def solution(mesh):
    placed = (
        P("grp", None, "ctx"),
        P("grp", None, "ctx"),
        P("grp", "ctx", None),
        P(None, "grp", None),
        P(None, "grp", None),
    )
    return jax.shard_map(
        functools.partial(body, mesh),
        mesh=mesh,
        in_specs=placed,
        out_specs=(
            P("grp", None, "ctx"),
            P("grp", "ctx", None),
            P(None, "grp", None),
            P(None, "grp", None),
        ),
        check_vma=False,
    )
```

```python
import functools
import math

import jax
import jax.numpy as jnp
import ml_dtypes
import numpy as np
from jax import lax
from jax.experimental import pallas as pl
from jax.experimental.pallas import tpu as pltpu
from jax.sharding import PartitionSpec as P

HIGH = lax.Precision.HIGHEST
BF16 = jnp.bfloat16
F32 = jnp.float32
TABLE_ENTRIES = 1 << 22
HALF = 256
VMEM_BYTES = 16 << 20


@functools.lru_cache(maxsize=None)
def dft_table(length):
    period = 2 * length
    phase = np.outer(np.arange(length), np.arange(length)) % period * (2.0 * np.pi / period)
    cos, sin = np.cos(phase), np.sin(phase)
    sin[:, 0] = 1.0 - 2.0 * (np.arange(length) % 2)
    half = min(HALF, length)
    both = np.stack([cos.reshape(length, -1, half), sin.reshape(length, -1, half)], axis=2)
    return both.reshape(length, period).astype(ml_dtypes.bfloat16)


def dot(left, right):
    return jnp.dot(left, right, preferred_element_type=F32)


def dot_nt(left, right):
    return lax.dot_general(left, right, (((1,), (1,)), ((), ())), preferred_element_type=F32)


def dot_tn(left, right):
    return lax.dot_general(left, right, (((0,), (0,)), ((), ())), preferred_element_type=F32)


def shape(dims, kind):
    return jax.ShapeDtypeStruct(dims, kind)


def own_index(offset):
    return jnp.bitwise_xor(lax.axis_index("ctx"), offset)


def part(index, size):
    return pl.ds(index * size if isinstance(index, int) else pl.multiple_of(index * size, size), size)


def cross_spectrum(first, left, right, half, scale):
    lc, ls, rc, rs = left[:, :half], left[:, half:], right[:, :half], right[:, half:]
    cc, ss = lc * rc, ls * rs
    real, imag = cc + ss, ls * rc - lc * rs
    if first:
        lane = lax.broadcasted_iota(jnp.int32, lc.shape, 1) == 0
        real = jnp.where(lane, 0.5 * cc, real)
        imag = jnp.where(lane, 0.5 * ss, imag)
    return jnp.concatenate([(scale * real).astype(BF16), (scale * imag).astype(BF16)], axis=1)


def blocks(table_ref):
    length, period = table_ref.shape
    width = 2 * min(HALF, length)
    return [slice(i, i + width) for i in range(0, period, width)]


def pack_kernel(chips, tok_ref, sibling_ref, *refs):
    pack_refs = refs[-chips:]
    chans = pack_refs[0].shape[1]
    for i, pack_ref in enumerate(pack_refs):
        rows = part(own_index(2 * i), chans)
        pack_ref[0] = tok_ref[rows, :]
        pack_ref[1] = sibling_ref[rows, :]


def unpack(pack_refs, signal):
    tokens = pack_refs[0].shape[2]
    for i, pack_ref in enumerate(pack_refs):
        for j in range(2):
            signal[:, part(own_index(2 * i + j), tokens)] = pack_ref[j]


def filter_spec_kernel(filt_ref, table_ref, spec_ref):
    spec_ref[...] = dot(filt_ref[...].astype(BF16), table_ref[...])


def rank_acts_kernel(down_ref, tok_ref, out_ref):
    out_ref[...] = dot(down_ref[...], tok_ref[...]).astype(BF16)


def grad_u_kernel(groups, filt_spec_ref, up_ref, acts_ref, table_ref, *refs):
    pack_refs, (spec_ref, keep_ref, give_ref, rank_ref, signal, cross, du) = refs[:-7], refs[-7:]
    length = table_ref.shape[0]
    chips = len(pack_refs)
    _, chans, tokens = pack_refs[0].shape
    unpack(pack_refs, signal)
    for cols in blocks(table_ref):
        half = (cols.stop - cols.start) // 2
        spec = dot(signal[...], table_ref[:, cols])
        spec_ref[:, cols] = spec.astype(BF16)
        cross[:, cols] = cross_spectrum(cols.start == 0, spec, filt_spec_ref[:, cols], half, 1.0 / length)
    grad_u = dot_nt(cross[...], table_ref[...]).astype(BF16)
    du[...] = grad_u
    rank = dot(up_ref[:, part(own_index(0), chans)], grad_u).astype(BF16)
    for i in range(2 * chips):
        for j in range(groups):
            rank_ref[i * groups + j, : rank.shape[0]] = rank[:, i * tokens : (i + 1) * tokens]
            rank_ref[i * groups + j, rank.shape[0] :] = acts_ref[...]
    for i in range(chips):
        for j, out_ref in enumerate((keep_ref, give_ref)):
            out_ref[i] = du[:, part(own_index(2 * i + j), tokens)]


def pairwise(values):
    while len(values) > 1:
        values = [values[i] + values[i + 1] for i in range(0, len(values), 2)]
    return values[0]


def du_pack_kernel(keep_ref, got_ref, *pack_refs):
    for i, pack_ref in enumerate(pack_refs):
        pack_ref[0] = keep_ref[i + 1]
        pack_ref[1] = got_ref[i + 1]


def rank_kernel(groups, scale, parts_ref, tok_ref, keep_ref, give_ref, rank_ref, acts_ref, adapter_ref):
    ranks, tokens = rank_ref.shape
    width = tok_ref.shape[0]
    shards = parts_ref.shape[0] // groups
    total = None
    for i in range(shards):
        both = parts_ref[i * groups].astype(F32)
        for j in range(1, groups):
            both = both + parts_ref[i * groups + j].astype(F32)
        acts_ref[:, i * tokens : (i + 1) * tokens] = both[ranks:].astype(BF16)
        total = both[:ranks] if total is None else total + both[:ranks]
    rank_grad = total.astype(BF16)
    rank_ref[...] = rank_grad
    adapter_ref[:, :width] = scale * dot_nt(rank_grad, tok_ref[...])
    up = None
    for i in range(shards // 2):
        for j, ref in enumerate((keep_ref, give_ref)):
            term = dot_nt(acts_ref[:, part(own_index(2 * i + j), tokens)], ref[i])
            up = term if up is None else up + term
    adapter_ref[:, width:] = scale * up


def chip_sum_kernel(own_ref, other_ref, out_ref):
    chans = out_ref.shape[1] - own_ref.shape[1]
    width = own_ref.shape[1] - chans
    out_ref[:, :width] = (own_ref[:, :width] + other_ref[:, :width]).astype(BF16)
    out_ref[:, width : width + chans] = own_ref[:, width:].astype(BF16)
    out_ref[:, width + chans :] = other_ref[:, width:].astype(BF16)


def filter_grad_kernel(acts_ref, up_ref, spec_ref, table_ref, *refs):
    pack_refs, (out_ref, signal, cross, out, sems) = refs[:-5], refs[-5:]
    length = table_ref.shape[0]
    chans = pack_refs[0].shape[1]
    unpack(pack_refs, signal)
    own_up = up_ref[:, part(own_index(0), chans)]
    act = (signal[...].astype(F32) + dot_tn(own_up, acts_ref[...])).astype(BF16)
    for cols in blocks(table_ref):
        half = (cols.stop - cols.start) // 2
        spec = dot(act, table_ref[:, cols])
        cross[:, cols] = cross_spectrum(cols.start == 0, spec_ref[:, cols].astype(F32), spec, half, 1.0 / length)
    copies = []
    for i in range(sems.shape[0]):
        lags = part(i, length // sems.shape[0])
        out[:, lags] = dot_nt(cross[...], table_ref[lags, :])
        copies.append(pltpu.make_async_copy(out.at[:, lags], out_ref.at[:, lags], sems.at[i]))
        copies[-1].start()
    for copy in copies:
        copy.wait()


def input_grad_kernel(keep_ref, got_ref, down_ref, rank_ref, *refs):
    pack_refs, out_ref = refs[:-1], refs[-1]
    chans = keep_ref.shape[1]

    def put(offset, value):
        index = own_index(offset)
        lift = dot_tn(down_ref[:, part(index, chans)], rank_ref[...])
        out_ref[part(index, chans), :] = (value.astype(F32) + lift).astype(BF16)

    put(0, keep_ref[0])
    put(1, got_ref[0])
    for i, pack_ref in enumerate(pack_refs):
        for j in range(2):
            put(2 * (i + 1) + j, pack_ref[j])


def adapter_sum_kernel(*refs):
    part_refs, down_out, up_out, total, chunks = refs[:-4], refs[-4], refs[-3], refs[-2], refs[-1]
    width = down_out.shape[2]
    chans = (part_refs[0].shape[1] - width) // 2
    down_out[:, 0, :] = pairwise([ref[:, :width].astype(F32) for ref in part_refs])
    for i, ref in enumerate(part_refs):
        for j in range(2):
            block = ref[:, width + j * chans : width + (j + 1) * chans]
            chunks[:, part(own_index(2 * i + j), chans)] = block.astype(F32)
    up_out[:, 0, :] = chunks[...]


def dense_body(mesh, saved_input, out_grad, filters, adapter_down, adapter_up):
    shards, groups = mesh.shape["ctx"], mesh.shape["grp"]
    tok_input, tok_grad, filt = saved_input[0], out_grad[0], filters[0]
    down, up = adapter_down[:, 0, :], adapter_up[:, 0, :]
    rank, width = down.shape
    tokens = tok_input.shape[1]
    chans, length = filt.shape
    chips = shards // 2
    table = jnp.asarray(dft_table(length))
    local = pl.BlockSpec(memory_space=pltpu.VMEM)
    product = 2 * chans * length * 2 * length

    def call(kernel, name, out_shape, args, scratch=(), flops=0, early=0, far_out=False):
        outs = jax.tree.leaves(out_shape)
        moved = sum(int(np.prod(o.shape)) * o.dtype.itemsize for o in outs)
        out_spec = pl.BlockSpec(memory_space=pl.ANY) if far_out else local
        out_specs = (out_spec,) * len(outs) if isinstance(out_shape, tuple) else out_spec
        return pl.pallas_call(
            kernel,
            out_shape=out_shape,
            in_specs=[local] * (len(args) - early) + [pl.BlockSpec(memory_space=pl.ANY)] * early,
            out_specs=out_specs,
            scratch_shapes=scratch,
            cost_estimate=pl.CostEstimate(flops=flops, bytes_accessed=moved, transcendentals=0),
            compiler_params=pltpu.CompilerParams(vmem_limit_bytes=VMEM_BYTES),
            name=name,
        )(*args)

    def send(value, offset, axis="ctx"):
        return lax.ppermute(value, axis, [(i, i ^ offset) for i in range(mesh.shape[axis])])

    def packed(own, sibling, name, early=(), flops=0):
        kernel = functools.partial(pack_kernel, chips)
        return call(kernel, name, (pack,) * chips, (own, sibling, *early), early=len(early), flops=flops)

    def to_chips(packs):
        return [packs[0]] + [send(packs[i], 2 * i) for i in range(1, chips)]

    vmem = pltpu.VMEM
    pack = shape((2, chans, tokens), BF16)
    sibling_grad = send(tok_grad, 1)
    sibling_input = send(tok_input, 1)
    ahead = 4 * product
    first = call(lambda out_ref: out_ref.__setitem__(Ellipsis, jnp.zeros_like(out_ref)), "first", shape((8, 128), F32), (), flops=ahead)
    grad_packs = packed(tok_grad, sibling_grad, "grad_pack", (first,), ahead)
    chan_grad = to_chips(grad_packs)
    everyone = shards * groups
    acts_part = call(rank_acts_kernel, "rank_acts", shape((rank, tokens), BF16), (down, tok_input))
    filt_spec = call(filter_spec_kernel, "filter_spec", shape((chans, 2 * length), F32), (filt, table), flops=product)
    half_du = shape((chips, chans, tokens), BF16)
    grad_spec, keep, give, rank_parts = call(
        functools.partial(grad_u_kernel, groups),
        "grad_u",
        (shape((chans, 2 * length), BF16), half_du, half_du, shape((everyone, 2 * rank, tokens), BF16)),
        (filt_spec, up, acts_part, table, *chan_grad),
        scratch=[vmem((chans, length), BF16), vmem((chans, 2 * length), BF16), vmem((chans, length), BF16)],
    )
    chan_packs = to_chips(packed(tok_input, sibling_input, "input_pack"))
    rank_parts, chan_packs = lax.optimization_barrier((rank_parts, chan_packs))
    all_parts = lax.all_to_all(rank_parts, ("ctx", "grp"), 0, 0, tiled=True)
    got = send(give, 1)
    du_packs = call(du_pack_kernel, "du_pack", (pack,) * (chips - 1), (keep, got))
    tok_packs = [send(du_packs[i], 2 * (i + 1)) for i in range(chips - 1)]
    all_parts, tok_packs = lax.optimization_barrier((all_parts, tok_packs))
    rank_grad, acts, adapter_part = call(
        functools.partial(rank_kernel, groups, float(length) ** -0.5),
        "rank_grad",
        (shape((rank, tokens), BF16), shape((rank, length), BF16), shape((rank, width + chans), F32)),
        (all_parts, tok_input, keep, give),
        flops=ahead,
    )
    grad_input = call(
        input_grad_kernel, "input_grad", shape((width, tokens), BF16), (keep, got, down, rank_grad, *tok_packs)
    )
    other_part, grad_input = lax.optimization_barrier((send(adapter_part, 1), grad_input))
    chip_part = call(
        chip_sum_kernel,
        "chip_sum",
        shape((rank, width + 2 * chans), BF16),
        (adapter_part, other_part),
    )
    chip_parts = [chip_part] + [send(chip_part, 2 * i) for i in range(1, chips)]
    filt_grad = call(
        filter_grad_kernel,
        "filter_grad",
        shape((chans, length), F32),
        (acts, up, grad_spec, table, *chan_packs),
        scratch=[
            vmem((chans, length), BF16),
            vmem((chans, 2 * length), BF16),
            vmem((chans, length), F32),
            pltpu.SemaphoreType.DMA((4,)),
        ],
        flops=2 * product,
        far_out=True,
    )
    grad_down, grad_up = call(
        adapter_sum_kernel,
        "adapter_sum",
        (shape((rank, 1, width), F32),) * 2,
        chip_parts,
        scratch=[pltpu.VMEM((rank, width), F32)] * 2,
    )
    return grad_input[None], filt_grad[None], grad_down, grad_up


def split_radix(points):
    radix_low = 1
    while (
        points % (radix_low * 2) == 0
        and radix_low * 2 * (radix_low * 2) <= points
        and (points // (radix_low * 2) % 2 == 0)
    ):
        radix_low = radix_low * 2
    return (radix_low, points // radix_low)


def angle_table(height, across, period):
    index_down = lax.broadcasted_iota(jnp.int32, (height, across), 0)
    index_across = lax.broadcasted_iota(jnp.int32, (height, across), 1)
    phase = (index_down * index_across % period).astype(jnp.float32) * (2.0 * math.pi / period)
    return (jnp.cos(phase), jnp.sin(phase))


def make_tables(points):
    radix_low, radix_high = split_radix(points)
    cos_one, sin_one = angle_table(radix_high, radix_high // 2, radix_high)
    first = jnp.concatenate([cos_one, -sin_one], axis=0)
    first_high = first.astype(jnp.bfloat16)
    first_low = (first - first_high.astype(jnp.float32)).astype(jnp.bfloat16)
    twist = angle_table(radix_high, radix_low, points)
    cos_two, sin_two = angle_table(radix_low, radix_low, radix_low)
    second_fwd = jnp.concatenate(
        [jnp.concatenate([cos_two, sin_two], axis=1), jnp.concatenate([-sin_two, cos_two], axis=1)],
        axis=0,
    )
    second_inv = jnp.concatenate(
        [jnp.concatenate([cos_two, -sin_two], axis=1), jnp.concatenate([sin_two, cos_two], axis=1)],
        axis=0,
    )
    last_inv = jnp.concatenate([cos_one, -sin_one], axis=0)
    return (
        radix_low,
        radix_high,
        first,
        first_high,
        first_low,
        twist,
        second_fwd,
        second_inv,
        last_inv,
    )


def forward_dft(signal, tables):
    radix_low, radix_high, first, first_high, first_low, twist, second_fwd, second_inv, last_inv = (
        tables
    )
    channels = signal.shape[0]
    blocks = signal.reshape(channels, radix_high // 2, radix_low)
    if signal.dtype == jnp.bfloat16:
        section_one = jnp.einsum(
            "kn,cnp->ckp", first_high, blocks, preferred_element_type=jnp.float32
        )
        section_one = section_one + jnp.einsum(
            "kn,cnp->ckp", first_low, blocks, preferred_element_type=jnp.float32
        )
    else:
        section_one = jnp.einsum("kn,cnp->ckp", first, blocks, precision=HIGH)
    real_one = section_one[:, :radix_high]
    imag_one = section_one[:, radix_high:]
    cos_twist, sin_twist = twist
    real_two = real_one * cos_twist + imag_one * sin_twist
    imag_two = imag_one * cos_twist - real_one * sin_twist
    joined = jnp.concatenate([real_two, imag_two], axis=2)
    spectrum = jnp.einsum("jq,ckq->cjk", second_fwd, joined, precision=HIGH)
    return (spectrum[:, :radix_low], spectrum[:, radix_low:])


def inverse_dft(spectrum, tables):
    radix_low, radix_high, first, first_high, first_low, twist, second_fwd, second_inv, last_inv = (
        tables
    )
    spec_real, spec_imag = spectrum
    channels = spec_real.shape[0]
    joined = jnp.concatenate([spec_real, spec_imag], axis=1)
    section_one = jnp.einsum("pq,cqk->cpk", second_inv, joined, precision=HIGH)
    real_one = section_one[:, :radix_low]
    imag_one = section_one[:, radix_low:]
    cos_twist = twist[0].T
    sin_twist = twist[1].T
    real_two = real_one * cos_twist - imag_one * sin_twist
    imag_two = real_one * sin_twist + imag_one * cos_twist
    stacked = jnp.concatenate([real_two, imag_two], axis=2)
    signal = jnp.einsum("kn,cpk->cnp", last_inv, stacked, precision=HIGH)
    return signal.reshape(channels, -1) / float(radix_low * radix_high)


def conj_product(spec_left, spec_right):
    left_real, left_imag = spec_left
    right_real, right_imag = spec_right
    return (
        left_real * right_real + left_imag * right_imag,
        left_imag * right_real - left_real * right_imag,
    )


def staged_body(saved_input, out_grad, filters, adapter_down, adapter_up):
    tok_input = saved_input[0]
    tok_grad = out_grad[0]
    down_rows = adapter_down[:, 0, :]
    up_float = adapter_up[:, 0, :].astype(jnp.float32)
    rank_part = jnp.dot(down_rows, tok_input, preferred_element_type=jnp.float32)
    rank_acts = lax.psum(rank_part, "grp")
    tok_act = (
        tok_input.astype(jnp.float32) + jnp.einsum("rc,rt->ct", up_float, rank_acts, precision=HIGH)
    ).astype(jnp.bfloat16)
    chan_act, chan_grad = (
        lax.all_to_all(tok_act, "ctx", split_axis=0, concat_axis=1, tiled=True),
        lax.all_to_all(tok_grad, "ctx", split_axis=0, concat_axis=1, tiled=True),
    )
    length = chan_act.shape[1]
    tables = make_tables(2 * length)
    act_spec = forward_dft(chan_act, tables)
    grad_spec = forward_dft(chan_grad, tables)
    kern_spec = forward_dft(filters[0], tables)
    chan_du = inverse_dft(conj_product(grad_spec, kern_spec), tables).astype(jnp.bfloat16)
    filt_grad = inverse_dft(conj_product(grad_spec, act_spec), tables)
    tok_du = lax.all_to_all(chan_du, "ctx", split_axis=1, concat_axis=0, tiled=True)
    du_float = tok_du.astype(jnp.float32)
    rank_grad = lax.psum(jnp.einsum("rc,ct->rt", up_float, du_float, precision=HIGH), "grp")
    grad_input = (
        du_float + jnp.einsum("rc,rt->ct", down_rows.astype(jnp.float32), rank_grad, precision=HIGH)
    ).astype(jnp.bfloat16)
    down_part = jnp.einsum("rt,ct->rc", rank_grad, tok_input.astype(jnp.float32), precision=HIGH)
    up_part = jnp.einsum("rt,ct->rc", rank_acts, du_float, precision=HIGH)
    down_sum, up_sum = lax.psum((down_part, up_part), "ctx")
    factor = float(length) ** (-0.5)
    return (
        grad_input[None],
        filt_grad[None],
        (factor * down_sum)[:, None, :],
        (factor * up_sum)[:, None, :],
    )


def body(mesh, saved_input, out_grad, filters, adapter_down, adapter_up):
    length = filters.shape[2]
    shards, groups = mesh.shape["ctx"], mesh.shape["grp"]
    paired = shards > 1 and shards & (shards - 1) == 0 and groups & (groups - 1) == 0
    if 2 * length * length <= TABLE_ENTRIES and paired:
        return dense_body(mesh, saved_input, out_grad, filters, adapter_down, adapter_up)
    return staged_body(saved_input, out_grad, filters, adapter_down, adapter_up)


def solution(mesh):
    placed = (
        P("grp", None, "ctx"),
        P("grp", None, "ctx"),
        P("grp", "ctx", None),
        P(None, "grp", None),
        P(None, "grp", None),
    )
    return jax.shard_map(
        functools.partial(body, mesh),
        mesh=mesh,
        in_specs=placed,
        out_specs=(
            P("grp", None, "ctx"),
            P("grp", "ctx", None),
            P(None, "grp", None),
            P(None, "grp", None),
        ),
        check_vma=False,
    )
```

```python
import functools
import math

import jax
import jax.numpy as jnp
import ml_dtypes
import numpy as np
from jax import lax
from jax.experimental import pallas as pl
from jax.experimental.pallas import tpu as pltpu
from jax.sharding import PartitionSpec as P

HIGH = lax.Precision.HIGHEST
BF16 = jnp.bfloat16
F32 = jnp.float32
TABLE_ENTRIES = 1 << 22
HALF = 256
VMEM_BYTES = 16 << 20


@functools.lru_cache(maxsize=None)
def dft_table(length):
    period = 2 * length
    phase = np.outer(np.arange(length), np.arange(length)) % period * (2.0 * np.pi / period)
    cos, sin = np.cos(phase), np.sin(phase)
    sin[:, 0] = 1.0 - 2.0 * (np.arange(length) % 2)
    half = min(HALF, length)
    both = np.stack([cos.reshape(length, -1, half), sin.reshape(length, -1, half)], axis=2)
    return both.reshape(length, period).astype(ml_dtypes.bfloat16)


def dot(left, right):
    return jnp.dot(left, right, preferred_element_type=F32)


def dot_nt(left, right):
    return lax.dot_general(left, right, (((1,), (1,)), ((), ())), preferred_element_type=F32)


def dot_tn(left, right):
    return lax.dot_general(left, right, (((0,), (0,)), ((), ())), preferred_element_type=F32)


def shape(dims, kind):
    return jax.ShapeDtypeStruct(dims, kind)


def own_index(offset):
    return jnp.bitwise_xor(lax.axis_index("ctx"), offset)


def chip_offset(slot, other=0, device=None):
    device = lax.axis_index("ctx") if device is None else device
    odd = jnp.bitwise_and(device, 1) ^ other
    return 2 * slot if slot not in (1, 2) else jnp.where(odd == 1, 2 * (3 - slot), 2 * slot)


def part(index, size):
    return pl.ds(index * size if isinstance(index, int) else pl.multiple_of(index * size, size), size)


def cross_spectrum(first, left, right, half, scale):
    lc, ls, rc, rs = left[:, :half], left[:, half:], right[:, :half], right[:, half:]
    cc, ss = lc * rc, ls * rs
    real, imag = cc + ss, ls * rc - lc * rs
    if first:
        lane = lax.broadcasted_iota(jnp.int32, lc.shape, 1) == 0
        real = jnp.where(lane, 0.5 * cc, real)
        imag = jnp.where(lane, 0.5 * ss, imag)
    return jnp.concatenate([(scale * real).astype(BF16), (scale * imag).astype(BF16)], axis=1)


def blocks(table_ref):
    length, period = table_ref.shape
    width = 2 * min(HALF, length)
    return [slice(i, i + width) for i in range(0, period, width)]


def pack_kernel(chips, tok_ref, sibling_ref, *refs):
    pack_refs = refs[-chips:]
    chans = pack_refs[0].shape[1]
    for i, pack_ref in enumerate(pack_refs):
        rows = part(own_index(chip_offset(i)), chans)
        pack_ref[0] = tok_ref[rows, :]
        pack_ref[1] = sibling_ref[rows, :]


def unpack(pack_refs, signal):
    tokens = pack_refs[0].shape[2]
    for i, pack_ref in enumerate(pack_refs):
        for j in range(2):
            signal[:, part(own_index(chip_offset(i) ^ j), tokens)] = pack_ref[j]


def filter_spec_kernel(filt_ref, table_ref, spec_ref):
    spec_ref[...] = dot(filt_ref[...].astype(BF16), table_ref[...])


def rank_acts_kernel(down_ref, tok_ref, out_ref):
    out_ref[...] = dot(down_ref[...], tok_ref[...]).astype(BF16)


def grad_u_kernel(groups, filt_spec_ref, up_ref, acts_ref, table_ref, *refs):
    pack_refs, (spec_ref, keep_ref, give_ref, rank_ref, signal, cross, du) = refs[:-7], refs[-7:]
    length = table_ref.shape[0]
    chips = len(pack_refs)
    _, chans, tokens = pack_refs[0].shape
    unpack(pack_refs, signal)
    for cols in blocks(table_ref):
        half = (cols.stop - cols.start) // 2
        spec = dot(signal[...], table_ref[:, cols])
        spec_ref[:, cols] = spec.astype(BF16)
        cross[:, cols] = cross_spectrum(cols.start == 0, spec, filt_spec_ref[:, cols], half, 1.0 / length)
    grad_u = dot_nt(cross[...], table_ref[...]).astype(BF16)
    du[...] = grad_u
    rank = dot(up_ref[:, part(own_index(0), chans)], grad_u).astype(BF16)
    for i in range(2 * chips):
        for j in range(groups):
            rank_ref[i * groups + j, : rank.shape[0]] = rank[:, i * tokens : (i + 1) * tokens]
            rank_ref[i * groups + j, rank.shape[0] :] = acts_ref[...]
    for i in range(chips):
        for j, out_ref in enumerate((keep_ref, give_ref)):
            out_ref[i] = du[:, part(own_index(chip_offset(i, j) ^ j), tokens)]


def pairwise(values):
    while len(values) > 1:
        values = [values[i] + values[i + 1] for i in range(0, len(values), 2)]
    return values[0]


def du_pack_kernel(keep_ref, got_ref, *pack_refs):
    for i, pack_ref in enumerate(pack_refs):
        pack_ref[0] = keep_ref[i + 1]
        pack_ref[1] = got_ref[i + 1]


def rank_kernel(groups, scale, parts_ref, tok_ref, keep_ref, give_ref, rank_ref, acts_ref, adapter_ref):
    ranks, tokens = rank_ref.shape
    width = tok_ref.shape[0]
    shards = parts_ref.shape[0] // groups
    total = None
    for i in range(shards):
        both = parts_ref[i * groups].astype(F32)
        for j in range(1, groups):
            both = both + parts_ref[i * groups + j].astype(F32)
        acts_ref[:, i * tokens : (i + 1) * tokens] = both[ranks:].astype(BF16)
        total = both[:ranks] if total is None else total + both[:ranks]
    rank_grad = total.astype(BF16)
    rank_ref[...] = rank_grad
    adapter_ref[:, :width] = scale * dot_nt(rank_grad, tok_ref[...])
    up = None
    for i in range(shards // 2):
        for j, ref in enumerate((keep_ref, give_ref)):
            term = dot_nt(acts_ref[:, part(own_index(chip_offset(i, j) ^ j), tokens)], ref[i])
            up = term if up is None else up + term
    adapter_ref[:, width:] = scale * up


def chip_sum_kernel(own_ref, other_ref, out_ref):
    chans = out_ref.shape[1] - own_ref.shape[1]
    width = own_ref.shape[1] - chans
    out_ref[:, :width] = (own_ref[:, :width] + other_ref[:, :width]).astype(BF16)
    out_ref[:, width : width + chans] = own_ref[:, width:].astype(BF16)
    out_ref[:, width + chans :] = other_ref[:, width:].astype(BF16)


def filter_grad_kernel(acts_ref, up_ref, spec_ref, table_ref, *refs):
    pack_refs, (out_ref, signal, cross, out, sems) = refs[:-5], refs[-5:]
    length = table_ref.shape[0]
    chans = pack_refs[0].shape[1]
    unpack(pack_refs, signal)
    own_up = up_ref[:, part(own_index(0), chans)]
    act = (signal[...].astype(F32) + dot_tn(own_up, acts_ref[...])).astype(BF16)
    for cols in blocks(table_ref):
        half = (cols.stop - cols.start) // 2
        spec = dot(act, table_ref[:, cols])
        cross[:, cols] = cross_spectrum(cols.start == 0, spec_ref[:, cols].astype(F32), spec, half, 1.0 / length)
    copies = []
    for i in range(sems.shape[0]):
        lags = part(i, length // sems.shape[0])
        out[:, lags] = dot_nt(cross[...], table_ref[lags, :])
        copies.append(pltpu.make_async_copy(out.at[:, lags], out_ref.at[:, lags], sems.at[i]))
        copies[-1].start()
    for copy in copies:
        copy.wait()


def input_grad_kernel(keep_ref, got_ref, down_ref, rank_ref, *refs):
    pack_refs, out_ref = refs[:-1], refs[-1]
    chans = keep_ref.shape[1]

    def put(offset, value):
        index = own_index(offset)
        lift = dot_tn(down_ref[:, part(index, chans)], rank_ref[...])
        out_ref[part(index, chans), :] = (value.astype(F32) + lift).astype(BF16)

    put(0, keep_ref[0])
    put(1, got_ref[0])
    for i, pack_ref in enumerate(pack_refs):
        for j in range(2):
            put(chip_offset(i + 1) ^ j, pack_ref[j])


def adapter_sum_kernel(*refs):
    part_refs, down_out, up_out, total, chunks = refs[:-4], refs[-4], refs[-3], refs[-2], refs[-1]
    width = down_out.shape[2]
    chans = (part_refs[0].shape[1] - width) // 2
    sums = [ref[:, :width].astype(F32) for ref in part_refs]
    if len(sums) > 2:
        odd = jnp.bitwise_and(lax.axis_index("ctx"), 1) == 1
        sums[1:3] = [jnp.where(odd, sums[2], sums[1]), jnp.where(odd, sums[1], sums[2])]
    down_out[:, 0, :] = pairwise(sums)
    for i, ref in enumerate(part_refs):
        for j in range(2):
            block = ref[:, width + j * chans : width + (j + 1) * chans]
            chunks[:, part(own_index(chip_offset(i) ^ j), chans)] = block.astype(F32)
    up_out[:, 0, :] = chunks[...]


def dense_body(mesh, saved_input, out_grad, filters, adapter_down, adapter_up):
    shards, groups = mesh.shape["ctx"], mesh.shape["grp"]
    tok_input, tok_grad, filt = saved_input[0], out_grad[0], filters[0]
    down, up = adapter_down[:, 0, :], adapter_up[:, 0, :]
    rank, width = down.shape
    tokens = tok_input.shape[1]
    chans, length = filt.shape
    chips = shards // 2
    table = jnp.asarray(dft_table(length))
    local = pl.BlockSpec(memory_space=pltpu.VMEM)
    product = 2 * chans * length * 2 * length

    def call(kernel, name, out_shape, args, scratch=(), flops=0, early=0, far_out=False):
        outs = jax.tree.leaves(out_shape)
        moved = sum(int(np.prod(o.shape)) * o.dtype.itemsize for o in outs)
        out_spec = pl.BlockSpec(memory_space=pl.ANY) if far_out else local
        out_specs = (out_spec,) * len(outs) if isinstance(out_shape, tuple) else out_spec
        return pl.pallas_call(
            kernel,
            out_shape=out_shape,
            in_specs=[local] * (len(args) - early) + [pl.BlockSpec(memory_space=pl.ANY)] * early,
            out_specs=out_specs,
            scratch_shapes=scratch,
            cost_estimate=pl.CostEstimate(flops=flops, bytes_accessed=moved, transcendentals=0),
            compiler_params=pltpu.CompilerParams(vmem_limit_bytes=VMEM_BYTES),
            name=name,
        )(*args)

    def send(value, offset, axis="ctx"):
        return lax.ppermute(value, axis, [(i, i ^ offset) for i in range(mesh.shape[axis])])

    def packed(own, sibling, name, early=(), flops=0):
        kernel = functools.partial(pack_kernel, chips)
        return call(kernel, name, (pack,) * chips, (own, sibling, *early), early=len(early), flops=flops)

    def to_chip(value, slot):
        other = slot if chips < 4 or slot not in (1, 2) else 3 - slot
        pairs = [(i, i ^ (2 * (other if i % 2 else slot))) for i in range(shards)]
        return lax.ppermute(value, "ctx", pairs)

    def to_chips(packs):
        return [packs[0]] + [to_chip(packs[i], i) for i in range(1, chips)]

    vmem = pltpu.VMEM
    pack = shape((2, chans, tokens), BF16)
    sibling_grad = send(tok_grad, 1)
    sibling_input = send(tok_input, 1)
    ahead = 4 * product
    first = call(lambda out_ref: out_ref.__setitem__(Ellipsis, jnp.zeros_like(out_ref)), "first", shape((8, 128), F32), (), flops=ahead)
    grad_packs = packed(tok_grad, sibling_grad, "grad_pack", (first,), ahead)
    chan_grad = to_chips(grad_packs)
    everyone = shards * groups
    acts_part = call(rank_acts_kernel, "rank_acts", shape((rank, tokens), BF16), (down, tok_input))
    filt_spec = call(filter_spec_kernel, "filter_spec", shape((chans, 2 * length), F32), (filt, table), flops=product)
    half_du = shape((chips, chans, tokens), BF16)
    grad_spec, keep, give, rank_parts = call(
        functools.partial(grad_u_kernel, groups),
        "grad_u",
        (shape((chans, 2 * length), BF16), half_du, half_du, shape((everyone, 2 * rank, tokens), BF16)),
        (filt_spec, up, acts_part, table, *chan_grad),
        scratch=[vmem((chans, length), BF16), vmem((chans, 2 * length), BF16), vmem((chans, length), BF16)],
    )
    chan_packs = to_chips(packed(tok_input, sibling_input, "input_pack"))
    late_pack = chan_packs.pop(2)
    rank_parts, chan_packs = lax.optimization_barrier((rank_parts, chan_packs))
    all_parts = lax.all_to_all(rank_parts, ("ctx", "grp"), 0, 0, tiled=True)
    got = send(give, 1)
    du_packs = call(du_pack_kernel, "du_pack", (pack,) * (chips - 1), (keep, got))
    tok_packs = [to_chip(du_packs[i], i + 1) for i in range(chips - 1)]
    all_parts, tok_packs, late_pack = lax.optimization_barrier((all_parts, tok_packs, late_pack))
    chan_packs.insert(2, late_pack)
    rank_grad, acts, adapter_part = call(
        functools.partial(rank_kernel, groups, float(length) ** -0.5),
        "rank_grad",
        (shape((rank, tokens), BF16), shape((rank, length), BF16), shape((rank, width + chans), F32)),
        (all_parts, tok_input, keep, give),
        flops=ahead,
    )
    grad_input = call(
        input_grad_kernel, "input_grad", shape((width, tokens), BF16), (keep, got, down, rank_grad, *tok_packs)
    )
    other_part, grad_input = lax.optimization_barrier((send(adapter_part, 1), grad_input))
    chip_part = call(
        chip_sum_kernel,
        "chip_sum",
        shape((rank, width + 2 * chans), BF16),
        (adapter_part, other_part),
    )
    chip_parts = to_chips([chip_part] * chips)
    filt_grad = call(
        filter_grad_kernel,
        "filter_grad",
        shape((chans, length), F32),
        (acts, up, grad_spec, table, *chan_packs),
        scratch=[
            vmem((chans, length), BF16),
            vmem((chans, 2 * length), BF16),
            vmem((chans, length), F32),
            pltpu.SemaphoreType.DMA((4,)),
        ],
        flops=2 * product,
        far_out=True,
    )
    grad_down, grad_up = call(
        adapter_sum_kernel,
        "adapter_sum",
        (shape((rank, 1, width), F32),) * 2,
        chip_parts,
        scratch=[pltpu.VMEM((rank, width), F32)] * 2,
    )
    return grad_input[None], filt_grad[None], grad_down, grad_up


def split_radix(points):
    radix_low = 1
    while (
        points % (radix_low * 2) == 0
        and radix_low * 2 * (radix_low * 2) <= points
        and (points // (radix_low * 2) % 2 == 0)
    ):
        radix_low = radix_low * 2
    return (radix_low, points // radix_low)


def angle_table(height, across, period):
    index_down = lax.broadcasted_iota(jnp.int32, (height, across), 0)
    index_across = lax.broadcasted_iota(jnp.int32, (height, across), 1)
    phase = (index_down * index_across % period).astype(jnp.float32) * (2.0 * math.pi / period)
    return (jnp.cos(phase), jnp.sin(phase))


def make_tables(points):
    radix_low, radix_high = split_radix(points)
    cos_one, sin_one = angle_table(radix_high, radix_high // 2, radix_high)
    first = jnp.concatenate([cos_one, -sin_one], axis=0)
    first_high = first.astype(jnp.bfloat16)
    first_low = (first - first_high.astype(jnp.float32)).astype(jnp.bfloat16)
    twist = angle_table(radix_high, radix_low, points)
    cos_two, sin_two = angle_table(radix_low, radix_low, radix_low)
    second_fwd = jnp.concatenate(
        [jnp.concatenate([cos_two, sin_two], axis=1), jnp.concatenate([-sin_two, cos_two], axis=1)],
        axis=0,
    )
    second_inv = jnp.concatenate(
        [jnp.concatenate([cos_two, -sin_two], axis=1), jnp.concatenate([sin_two, cos_two], axis=1)],
        axis=0,
    )
    last_inv = jnp.concatenate([cos_one, -sin_one], axis=0)
    return (
        radix_low,
        radix_high,
        first,
        first_high,
        first_low,
        twist,
        second_fwd,
        second_inv,
        last_inv,
    )


def forward_dft(signal, tables):
    radix_low, radix_high, first, first_high, first_low, twist, second_fwd, second_inv, last_inv = (
        tables
    )
    channels = signal.shape[0]
    blocks = signal.reshape(channels, radix_high // 2, radix_low)
    if signal.dtype == jnp.bfloat16:
        section_one = jnp.einsum(
            "kn,cnp->ckp", first_high, blocks, preferred_element_type=jnp.float32
        )
        section_one = section_one + jnp.einsum(
            "kn,cnp->ckp", first_low, blocks, preferred_element_type=jnp.float32
        )
    else:
        section_one = jnp.einsum("kn,cnp->ckp", first, blocks, precision=HIGH)
    real_one = section_one[:, :radix_high]
    imag_one = section_one[:, radix_high:]
    cos_twist, sin_twist = twist
    real_two = real_one * cos_twist + imag_one * sin_twist
    imag_two = imag_one * cos_twist - real_one * sin_twist
    joined = jnp.concatenate([real_two, imag_two], axis=2)
    spectrum = jnp.einsum("jq,ckq->cjk", second_fwd, joined, precision=HIGH)
    return (spectrum[:, :radix_low], spectrum[:, radix_low:])


def inverse_dft(spectrum, tables):
    radix_low, radix_high, first, first_high, first_low, twist, second_fwd, second_inv, last_inv = (
        tables
    )
    spec_real, spec_imag = spectrum
    channels = spec_real.shape[0]
    joined = jnp.concatenate([spec_real, spec_imag], axis=1)
    section_one = jnp.einsum("pq,cqk->cpk", second_inv, joined, precision=HIGH)
    real_one = section_one[:, :radix_low]
    imag_one = section_one[:, radix_low:]
    cos_twist = twist[0].T
    sin_twist = twist[1].T
    real_two = real_one * cos_twist - imag_one * sin_twist
    imag_two = real_one * sin_twist + imag_one * cos_twist
    stacked = jnp.concatenate([real_two, imag_two], axis=2)
    signal = jnp.einsum("kn,cpk->cnp", last_inv, stacked, precision=HIGH)
    return signal.reshape(channels, -1) / float(radix_low * radix_high)


def conj_product(spec_left, spec_right):
    left_real, left_imag = spec_left
    right_real, right_imag = spec_right
    return (
        left_real * right_real + left_imag * right_imag,
        left_imag * right_real - left_real * right_imag,
    )


def staged_body(saved_input, out_grad, filters, adapter_down, adapter_up):
    tok_input = saved_input[0]
    tok_grad = out_grad[0]
    down_rows = adapter_down[:, 0, :]
    up_float = adapter_up[:, 0, :].astype(jnp.float32)
    rank_part = jnp.dot(down_rows, tok_input, preferred_element_type=jnp.float32)
    rank_acts = lax.psum(rank_part, "grp")
    tok_act = (
        tok_input.astype(jnp.float32) + jnp.einsum("rc,rt->ct", up_float, rank_acts, precision=HIGH)
    ).astype(jnp.bfloat16)
    chan_act, chan_grad = (
        lax.all_to_all(tok_act, "ctx", split_axis=0, concat_axis=1, tiled=True),
        lax.all_to_all(tok_grad, "ctx", split_axis=0, concat_axis=1, tiled=True),
    )
    length = chan_act.shape[1]
    tables = make_tables(2 * length)
    act_spec = forward_dft(chan_act, tables)
    grad_spec = forward_dft(chan_grad, tables)
    kern_spec = forward_dft(filters[0], tables)
    chan_du = inverse_dft(conj_product(grad_spec, kern_spec), tables).astype(jnp.bfloat16)
    filt_grad = inverse_dft(conj_product(grad_spec, act_spec), tables)
    tok_du = lax.all_to_all(chan_du, "ctx", split_axis=1, concat_axis=0, tiled=True)
    du_float = tok_du.astype(jnp.float32)
    rank_grad = lax.psum(jnp.einsum("rc,ct->rt", up_float, du_float, precision=HIGH), "grp")
    grad_input = (
        du_float + jnp.einsum("rc,rt->ct", down_rows.astype(jnp.float32), rank_grad, precision=HIGH)
    ).astype(jnp.bfloat16)
    down_part = jnp.einsum("rt,ct->rc", rank_grad, tok_input.astype(jnp.float32), precision=HIGH)
    up_part = jnp.einsum("rt,ct->rc", rank_acts, du_float, precision=HIGH)
    down_sum, up_sum = lax.psum((down_part, up_part), "ctx")
    factor = float(length) ** (-0.5)
    return (
        grad_input[None],
        filt_grad[None],
        (factor * down_sum)[:, None, :],
        (factor * up_sum)[:, None, :],
    )


def body(mesh, saved_input, out_grad, filters, adapter_down, adapter_up):
    length = filters.shape[2]
    shards, groups = mesh.shape["ctx"], mesh.shape["grp"]
    paired = shards > 1 and shards & (shards - 1) == 0 and groups & (groups - 1) == 0
    if 2 * length * length <= TABLE_ENTRIES and paired:
        return dense_body(mesh, saved_input, out_grad, filters, adapter_down, adapter_up)
    return staged_body(saved_input, out_grad, filters, adapter_down, adapter_up)


def solution(mesh):
    placed = (
        P("grp", None, "ctx"),
        P("grp", None, "ctx"),
        P("grp", "ctx", None),
        P(None, "grp", None),
        P(None, "grp", None),
    )
    return jax.shard_map(
        functools.partial(body, mesh),
        mesh=mesh,
        in_specs=placed,
        out_specs=(
            P("grp", None, "ctx"),
            P("grp", "ctx", None),
            P(None, "grp", None),
            P(None, "grp", None),
        ),
        check_vma=False,
    )
```

```python
import functools
import math

import jax
import jax.numpy as jnp
import ml_dtypes
import numpy as np
from jax import lax
from jax.experimental import pallas as pl
from jax.experimental.pallas import tpu as pltpu
from jax.sharding import PartitionSpec as P

HIGH = lax.Precision.HIGHEST
BF16 = jnp.bfloat16
F32 = jnp.float32
TABLE_ENTRIES = 1 << 22
HALF = 256
VMEM_BYTES = 16 << 20


@functools.lru_cache(maxsize=None)
def dft_table(length):
    period = 2 * length
    phase = np.outer(np.arange(length), np.arange(length)) % period * (2.0 * np.pi / period)
    cos, sin = np.cos(phase), np.sin(phase)
    sin[:, 0] = 1.0 - 2.0 * (np.arange(length) % 2)
    half = min(HALF, length)
    both = np.stack([cos.reshape(length, -1, half), sin.reshape(length, -1, half)], axis=2)
    return both.reshape(length, period).astype(ml_dtypes.bfloat16)


def dot(left, right):
    return jnp.dot(left, right, preferred_element_type=F32)


def dot_nt(left, right):
    return lax.dot_general(left, right, (((1,), (1,)), ((), ())), preferred_element_type=F32)


def dot_tn(left, right):
    return lax.dot_general(left, right, (((0,), (0,)), ((), ())), preferred_element_type=F32)


def shape(dims, kind):
    return jax.ShapeDtypeStruct(dims, kind)


def own_index(offset):
    return jnp.bitwise_xor(lax.axis_index("ctx"), offset)


def chip_offset(slot, other=0, device=None):
    device = lax.axis_index("ctx") if device is None else device
    odd = jnp.bitwise_and(device, 1) ^ other
    return 2 * slot if slot not in (1, 2) else jnp.where(odd == 1, 2 * (3 - slot), 2 * slot)


def part(index, size):
    return pl.ds(index * size if isinstance(index, int) else pl.multiple_of(index * size, size), size)


def cross_spectrum(first, left, right, half, scale):
    lc, ls, rc, rs = left[:, :half], left[:, half:], right[:, :half], right[:, half:]
    cc, ss = lc * rc, ls * rs
    real, imag = cc + ss, ls * rc - lc * rs
    if first:
        lane = lax.broadcasted_iota(jnp.int32, lc.shape, 1) == 0
        real = jnp.where(lane, 0.5 * cc, real)
        imag = jnp.where(lane, 0.5 * ss, imag)
    return jnp.concatenate([(scale * real).astype(BF16), (scale * imag).astype(BF16)], axis=1)


def blocks(table_ref):
    length, period = table_ref.shape
    width = 2 * min(HALF, length)
    return [slice(i, i + width) for i in range(0, period, width)]


def pack_kernel(chips, tok_ref, sibling_ref, *refs):
    pack_refs = refs[-chips:]
    chans = pack_refs[0].shape[1]
    for i, pack_ref in enumerate(pack_refs):
        rows = part(own_index(chip_offset(i)), chans)
        pack_ref[0] = tok_ref[rows, :]
        pack_ref[1] = sibling_ref[rows, :]


def unpack(pack_refs, signal):
    tokens = pack_refs[0].shape[2]
    for i, pack_ref in enumerate(pack_refs):
        for j in range(2):
            signal[:, part(own_index(chip_offset(i) ^ j), tokens)] = pack_ref[j]


def filter_spec_kernel(filt_ref, table_ref, spec_ref):
    spec_ref[...] = dot(filt_ref[...].astype(BF16), table_ref[...])


def rank_acts_kernel(down_ref, tok_ref, out_ref):
    out_ref[...] = dot(down_ref[...], tok_ref[...]).astype(BF16)


def grad_u_kernel(groups, filt_spec_ref, up_ref, acts_ref, table_ref, *refs):
    pack_refs, (spec_ref, keep_ref, give_ref, rank_ref, signal, cross, du) = refs[:-7], refs[-7:]
    length = table_ref.shape[0]
    chips = len(pack_refs)
    _, chans, tokens = pack_refs[0].shape
    unpack(pack_refs, signal)
    for cols in blocks(table_ref):
        half = (cols.stop - cols.start) // 2
        spec = dot(signal[...], table_ref[:, cols])
        spec_ref[:, cols] = spec.astype(BF16)
        cross[:, cols] = cross_spectrum(cols.start == 0, spec, filt_spec_ref[:, cols], half, 1.0 / length)
    grad_u = dot_nt(cross[...], table_ref[...]).astype(BF16)
    du[...] = grad_u
    rank = dot(up_ref[:, part(own_index(0), chans)], grad_u).astype(BF16)
    for i in range(2 * chips):
        for j in range(groups):
            rank_ref[i * groups + j, : rank.shape[0]] = rank[:, i * tokens : (i + 1) * tokens]
            rank_ref[i * groups + j, rank.shape[0] :] = acts_ref[...]
    for i in range(chips):
        for j, out_ref in enumerate((keep_ref, give_ref)):
            out_ref[i] = du[:, part(own_index(chip_offset(i, j) ^ j), tokens)]


def pairwise(values):
    while len(values) > 1:
        values = [values[i] + values[i + 1] for i in range(0, len(values), 2)]
    return values[0]


def du_pack_kernel(keep_ref, got_ref, *pack_refs):
    for i, pack_ref in enumerate(pack_refs):
        pack_ref[0] = keep_ref[i + 1]
        pack_ref[1] = got_ref[i + 1]


def rank_kernel(groups, scale, parts_ref, tok_ref, keep_ref, give_ref, rank_ref, acts_ref, adapter_ref):
    ranks, tokens = rank_ref.shape
    width = tok_ref.shape[0]
    shards = parts_ref.shape[0] // groups
    total = None
    for i in range(shards):
        both = parts_ref[i * groups].astype(F32)
        for j in range(1, groups):
            both = both + parts_ref[i * groups + j].astype(F32)
        acts_ref[:, i * tokens : (i + 1) * tokens] = both[ranks:].astype(BF16)
        total = both[:ranks] if total is None else total + both[:ranks]
    rank_grad = total.astype(BF16)
    rank_ref[...] = rank_grad
    adapter_ref[:, :width] = scale * dot_nt(rank_grad, tok_ref[...])
    up = None
    for i in range(shards // 2):
        for j, ref in enumerate((keep_ref, give_ref)):
            term = dot_nt(acts_ref[:, part(own_index(chip_offset(i, j) ^ j), tokens)], ref[i])
            up = term if up is None else up + term
    adapter_ref[:, width:] = scale * up


def chip_sum_kernel(own_ref, other_ref, out_ref):
    chans = out_ref.shape[1] - own_ref.shape[1]
    width = own_ref.shape[1] - chans
    out_ref[:, :width] = (own_ref[:, :width] + other_ref[:, :width]).astype(BF16)
    out_ref[:, width : width + chans] = own_ref[:, width:].astype(BF16)
    out_ref[:, width + chans :] = other_ref[:, width:].astype(BF16)


def filter_grad_kernel(acts_ref, up_ref, spec_ref, table_ref, *refs):
    pack_refs, (out_ref, signal, cross, out, sems) = refs[:-5], refs[-5:]
    length = table_ref.shape[0]
    chans = pack_refs[0].shape[1]
    unpack(pack_refs, signal)
    own_up = up_ref[:, part(own_index(0), chans)]
    act = (signal[...].astype(F32) + dot_tn(own_up, acts_ref[...])).astype(BF16)
    for cols in blocks(table_ref):
        half = (cols.stop - cols.start) // 2
        spec = dot(act, table_ref[:, cols])
        cross[:, cols] = cross_spectrum(cols.start == 0, spec_ref[:, cols].astype(F32), spec, half, 1.0 / length)
    copies = []
    for i in range(sems.shape[0]):
        lags = part(i, length // sems.shape[0])
        out[:, lags] = dot_nt(cross[...], table_ref[lags, :])
        copies.append(pltpu.make_async_copy(out.at[:, lags], out_ref.at[:, lags], sems.at[i]))
        copies[-1].start()
    for copy in copies:
        copy.wait()


def input_grad_kernel(keep_ref, got_ref, down_ref, rank_ref, *refs):
    pack_refs, out_ref = refs[:-1], refs[-1]
    chans = keep_ref.shape[1]

    def put(offset, value):
        index = own_index(offset)
        lift = dot_tn(down_ref[:, part(index, chans)], rank_ref[...])
        out_ref[part(index, chans), :] = (value.astype(F32) + lift).astype(BF16)

    put(0, keep_ref[0])
    put(1, got_ref[0])
    for i, pack_ref in enumerate(pack_refs):
        for j in range(2):
            put(chip_offset(i + 1) ^ j, pack_ref[j])


def adapter_sum_kernel(*refs):
    part_refs, down_out, up_out, total, chunks = refs[:-4], refs[-4], refs[-3], refs[-2], refs[-1]
    width = down_out.shape[2]
    chans = (part_refs[0].shape[1] - width) // 2
    sums = [ref[:, :width].astype(F32) for ref in part_refs]
    if len(sums) > 2:
        odd = jnp.bitwise_and(lax.axis_index("ctx"), 1) == 1
        sums[1:3] = [jnp.where(odd, sums[2], sums[1]), jnp.where(odd, sums[1], sums[2])]
    down_out[:, 0, :] = pairwise(sums)
    for i, ref in enumerate(part_refs):
        for j in range(2):
            block = ref[:, width + j * chans : width + (j + 1) * chans]
            chunks[:, part(own_index(chip_offset(i) ^ j), chans)] = block.astype(F32)
    up_out[:, 0, :] = chunks[...]


def dense_body(mesh, saved_input, out_grad, filters, adapter_down, adapter_up):
    shards, groups = mesh.shape["ctx"], mesh.shape["grp"]
    tok_input, tok_grad, filt = saved_input[0], out_grad[0], filters[0]
    down, up = adapter_down[:, 0, :], adapter_up[:, 0, :]
    rank, width = down.shape
    tokens = tok_input.shape[1]
    chans, length = filt.shape
    chips = shards // 2
    table = jnp.asarray(dft_table(length))
    local = pl.BlockSpec(memory_space=pltpu.VMEM)
    product = 2 * chans * length * 2 * length

    def call(kernel, name, out_shape, args, scratch=(), flops=0, early=0, far_out=False):
        outs = jax.tree.leaves(out_shape)
        moved = sum(int(np.prod(o.shape)) * o.dtype.itemsize for o in outs)
        out_spec = pl.BlockSpec(memory_space=pl.ANY) if far_out else local
        out_specs = (out_spec,) * len(outs) if isinstance(out_shape, tuple) else out_spec
        return pl.pallas_call(
            kernel,
            out_shape=out_shape,
            in_specs=[local] * (len(args) - early) + [pl.BlockSpec(memory_space=pl.ANY)] * early,
            out_specs=out_specs,
            scratch_shapes=scratch,
            cost_estimate=pl.CostEstimate(flops=flops, bytes_accessed=moved, transcendentals=0),
            compiler_params=pltpu.CompilerParams(vmem_limit_bytes=VMEM_BYTES),
            name=name,
        )(*args)

    def send(value, offset, axis="ctx"):
        return lax.ppermute(value, axis, [(i, i ^ offset) for i in range(mesh.shape[axis])])

    def packed(own, sibling, name, early=(), flops=0):
        kernel = functools.partial(pack_kernel, chips)
        return call(kernel, name, (pack,) * chips, (own, sibling, *early), early=len(early), flops=flops)

    def to_chip(value, slot):
        other = slot if chips < 4 or slot not in (1, 2) else 3 - slot
        pairs = [(i, i ^ (2 * (other if i % 2 else slot))) for i in range(shards)]
        return lax.ppermute(value, "ctx", pairs)

    def to_chips(packs):
        return [packs[0]] + [to_chip(packs[i], i) for i in range(1, chips)]

    vmem = pltpu.VMEM
    pack = shape((2, chans, tokens), BF16)
    sibling_grad = send(tok_grad, 1)
    sibling_input = send(tok_input, 1)
    ahead = 4 * product
    first = call(lambda out_ref: out_ref.__setitem__(Ellipsis, jnp.zeros_like(out_ref)), "first", shape((8, 128), F32), (), flops=ahead)
    grad_packs = packed(tok_grad, sibling_grad, "grad_pack", (first,), ahead)
    chan_grad = to_chips(grad_packs)
    everyone = shards * groups
    acts_part = call(rank_acts_kernel, "rank_acts", shape((rank, tokens), BF16), (down, tok_input))
    filt_spec = call(filter_spec_kernel, "filter_spec", shape((chans, 2 * length), F32), (filt, table), flops=product)
    half_du = shape((chips, chans, tokens), BF16)
    grad_spec, keep, give, rank_parts = call(
        functools.partial(grad_u_kernel, groups),
        "grad_u",
        (shape((chans, 2 * length), BF16), half_du, half_du, shape((everyone, 2 * rank, tokens), BF16)),
        (filt_spec, up, acts_part, table, *chan_grad),
        scratch=[vmem((chans, length), BF16), vmem((chans, 2 * length), BF16), vmem((chans, length), BF16)],
    )
    chan_packs = to_chips(packed(tok_input, sibling_input, "input_pack"))
    late_pack = chan_packs.pop(1)
    rank_parts, chan_packs = lax.optimization_barrier((rank_parts, chan_packs))
    all_parts = lax.all_to_all(rank_parts, ("ctx", "grp"), 0, 0, tiled=True)
    got = send(give, 1)
    du_packs = call(du_pack_kernel, "du_pack", (pack,) * (chips - 1), (keep, got))
    tok_packs = [to_chip(du_packs[i], i + 1) for i in range(chips - 1)]
    all_parts, tok_packs[:2], late_pack = lax.optimization_barrier((all_parts, tok_packs[:2], late_pack))
    chan_packs.insert(1, late_pack)
    rank_grad, acts, adapter_part = call(
        functools.partial(rank_kernel, groups, float(length) ** -0.5),
        "rank_grad",
        (shape((rank, tokens), BF16), shape((rank, length), BF16), shape((rank, width + chans), F32)),
        (all_parts, tok_input, keep, give),
        flops=ahead,
    )
    other_part = send(adapter_part, 1)
    chip_part = call(
        chip_sum_kernel,
        "chip_sum",
        shape((rank, width + 2 * chans), BF16),
        (adapter_part, other_part),
    )
    chip_parts = to_chips([chip_part] * chips)
    filt_grad = call(
        filter_grad_kernel,
        "filter_grad",
        shape((chans, length), F32),
        (acts, up, grad_spec, table, *chan_packs),
        scratch=[
            vmem((chans, length), BF16),
            vmem((chans, 2 * length), BF16),
            vmem((chans, length), F32),
            pltpu.SemaphoreType.DMA((2,)),
        ],
        flops=2 * product,
        far_out=True,
    )
    filt_grad, got = lax.optimization_barrier((filt_grad, got))
    grad_input = call(
        input_grad_kernel, "input_grad", shape((width, tokens), BF16), (keep, got, down, rank_grad, *tok_packs)
    )
    grad_down, grad_up = call(
        adapter_sum_kernel,
        "adapter_sum",
        (shape((rank, 1, width), F32),) * 2,
        chip_parts,
        scratch=[pltpu.VMEM((rank, width), F32)] * 2,
    )
    return grad_input[None], filt_grad[None], grad_down, grad_up


def split_radix(points):
    radix_low = 1
    while (
        points % (radix_low * 2) == 0
        and radix_low * 2 * (radix_low * 2) <= points
        and (points // (radix_low * 2) % 2 == 0)
    ):
        radix_low = radix_low * 2
    return (radix_low, points // radix_low)


def angle_table(height, across, period):
    index_down = lax.broadcasted_iota(jnp.int32, (height, across), 0)
    index_across = lax.broadcasted_iota(jnp.int32, (height, across), 1)
    phase = (index_down * index_across % period).astype(jnp.float32) * (2.0 * math.pi / period)
    return (jnp.cos(phase), jnp.sin(phase))


def make_tables(points):
    radix_low, radix_high = split_radix(points)
    cos_one, sin_one = angle_table(radix_high, radix_high // 2, radix_high)
    first = jnp.concatenate([cos_one, -sin_one], axis=0)
    first_high = first.astype(jnp.bfloat16)
    first_low = (first - first_high.astype(jnp.float32)).astype(jnp.bfloat16)
    twist = angle_table(radix_high, radix_low, points)
    cos_two, sin_two = angle_table(radix_low, radix_low, radix_low)
    second_fwd = jnp.concatenate(
        [jnp.concatenate([cos_two, sin_two], axis=1), jnp.concatenate([-sin_two, cos_two], axis=1)],
        axis=0,
    )
    second_inv = jnp.concatenate(
        [jnp.concatenate([cos_two, -sin_two], axis=1), jnp.concatenate([sin_two, cos_two], axis=1)],
        axis=0,
    )
    last_inv = jnp.concatenate([cos_one, -sin_one], axis=0)
    return (
        radix_low,
        radix_high,
        first,
        first_high,
        first_low,
        twist,
        second_fwd,
        second_inv,
        last_inv,
    )


def forward_dft(signal, tables):
    radix_low, radix_high, first, first_high, first_low, twist, second_fwd, second_inv, last_inv = (
        tables
    )
    channels = signal.shape[0]
    blocks = signal.reshape(channels, radix_high // 2, radix_low)
    if signal.dtype == jnp.bfloat16:
        section_one = jnp.einsum(
            "kn,cnp->ckp", first_high, blocks, preferred_element_type=jnp.float32
        )
        section_one = section_one + jnp.einsum(
            "kn,cnp->ckp", first_low, blocks, preferred_element_type=jnp.float32
        )
    else:
        section_one = jnp.einsum("kn,cnp->ckp", first, blocks, precision=HIGH)
    real_one = section_one[:, :radix_high]
    imag_one = section_one[:, radix_high:]
    cos_twist, sin_twist = twist
    real_two = real_one * cos_twist + imag_one * sin_twist
    imag_two = imag_one * cos_twist - real_one * sin_twist
    joined = jnp.concatenate([real_two, imag_two], axis=2)
    spectrum = jnp.einsum("jq,ckq->cjk", second_fwd, joined, precision=HIGH)
    return (spectrum[:, :radix_low], spectrum[:, radix_low:])


def inverse_dft(spectrum, tables):
    radix_low, radix_high, first, first_high, first_low, twist, second_fwd, second_inv, last_inv = (
        tables
    )
    spec_real, spec_imag = spectrum
    channels = spec_real.shape[0]
    joined = jnp.concatenate([spec_real, spec_imag], axis=1)
    section_one = jnp.einsum("pq,cqk->cpk", second_inv, joined, precision=HIGH)
    real_one = section_one[:, :radix_low]
    imag_one = section_one[:, radix_low:]
    cos_twist = twist[0].T
    sin_twist = twist[1].T
    real_two = real_one * cos_twist - imag_one * sin_twist
    imag_two = real_one * sin_twist + imag_one * cos_twist
    stacked = jnp.concatenate([real_two, imag_two], axis=2)
    signal = jnp.einsum("kn,cpk->cnp", last_inv, stacked, precision=HIGH)
    return signal.reshape(channels, -1) / float(radix_low * radix_high)


def conj_product(spec_left, spec_right):
    left_real, left_imag = spec_left
    right_real, right_imag = spec_right
    return (
        left_real * right_real + left_imag * right_imag,
        left_imag * right_real - left_real * right_imag,
    )


def staged_body(saved_input, out_grad, filters, adapter_down, adapter_up):
    tok_input = saved_input[0]
    tok_grad = out_grad[0]
    down_rows = adapter_down[:, 0, :]
    up_float = adapter_up[:, 0, :].astype(jnp.float32)
    rank_part = jnp.dot(down_rows, tok_input, preferred_element_type=jnp.float32)
    rank_acts = lax.psum(rank_part, "grp")
    tok_act = (
        tok_input.astype(jnp.float32) + jnp.einsum("rc,rt->ct", up_float, rank_acts, precision=HIGH)
    ).astype(jnp.bfloat16)
    chan_act, chan_grad = (
        lax.all_to_all(tok_act, "ctx", split_axis=0, concat_axis=1, tiled=True),
        lax.all_to_all(tok_grad, "ctx", split_axis=0, concat_axis=1, tiled=True),
    )
    length = chan_act.shape[1]
    tables = make_tables(2 * length)
    act_spec = forward_dft(chan_act, tables)
    grad_spec = forward_dft(chan_grad, tables)
    kern_spec = forward_dft(filters[0], tables)
    chan_du = inverse_dft(conj_product(grad_spec, kern_spec), tables).astype(jnp.bfloat16)
    filt_grad = inverse_dft(conj_product(grad_spec, act_spec), tables)
    tok_du = lax.all_to_all(chan_du, "ctx", split_axis=1, concat_axis=0, tiled=True)
    du_float = tok_du.astype(jnp.float32)
    rank_grad = lax.psum(jnp.einsum("rc,ct->rt", up_float, du_float, precision=HIGH), "grp")
    grad_input = (
        du_float + jnp.einsum("rc,rt->ct", down_rows.astype(jnp.float32), rank_grad, precision=HIGH)
    ).astype(jnp.bfloat16)
    down_part = jnp.einsum("rt,ct->rc", rank_grad, tok_input.astype(jnp.float32), precision=HIGH)
    up_part = jnp.einsum("rt,ct->rc", rank_acts, du_float, precision=HIGH)
    down_sum, up_sum = lax.psum((down_part, up_part), "ctx")
    factor = float(length) ** (-0.5)
    return (
        grad_input[None],
        filt_grad[None],
        (factor * down_sum)[:, None, :],
        (factor * up_sum)[:, None, :],
    )


def body(mesh, saved_input, out_grad, filters, adapter_down, adapter_up):
    length = filters.shape[2]
    shards, groups = mesh.shape["ctx"], mesh.shape["grp"]
    paired = shards > 1 and shards & (shards - 1) == 0 and groups & (groups - 1) == 0
    if 2 * length * length <= TABLE_ENTRIES and paired:
        return dense_body(mesh, saved_input, out_grad, filters, adapter_down, adapter_up)
    return staged_body(saved_input, out_grad, filters, adapter_down, adapter_up)


def solution(mesh):
    placed = (
        P("grp", None, "ctx"),
        P("grp", None, "ctx"),
        P("grp", "ctx", None),
        P(None, "grp", None),
        P(None, "grp", None),
    )
    return jax.shard_map(
        functools.partial(body, mesh),
        mesh=mesh,
        in_specs=placed,
        out_specs=(
            P("grp", None, "ctx"),
            P("grp", "ctx", None),
            P(None, "grp", None),
            P(None, "grp", None),
        ),
        check_vma=False,
    )
```

```python
import functools
import math

import jax
import jax.numpy as jnp
import ml_dtypes
import numpy as np
from jax import lax
from jax.experimental import pallas as pl
from jax.experimental.pallas import tpu as pltpu
from jax.sharding import PartitionSpec as P

HIGH = lax.Precision.HIGHEST
BF16 = jnp.bfloat16
F32 = jnp.float32
TABLE_ENTRIES = 1 << 22
HALF = 256
VMEM_BYTES = 16 << 20


@functools.lru_cache(maxsize=None)
def dft_table(length):
    period = 2 * length
    phase = np.outer(np.arange(length), np.arange(length)) % period * (2.0 * np.pi / period)
    cos, sin = np.cos(phase), np.sin(phase)
    sin[:, 0] = 1.0 - 2.0 * (np.arange(length) % 2)
    half = min(HALF, length)
    both = np.stack([cos.reshape(length, -1, half), sin.reshape(length, -1, half)], axis=2)
    return both.reshape(length, period).astype(ml_dtypes.bfloat16)


def dot(left, right):
    return jnp.dot(left, right, preferred_element_type=F32)


def dot_nt(left, right):
    return lax.dot_general(left, right, (((1,), (1,)), ((), ())), preferred_element_type=F32)


def dot_tn(left, right):
    return lax.dot_general(left, right, (((0,), (0,)), ((), ())), preferred_element_type=F32)


def shape(dims, kind):
    return jax.ShapeDtypeStruct(dims, kind)


def own_index(offset):
    return jnp.bitwise_xor(lax.axis_index("ctx"), offset)


def chip_offset(slot, other=0, device=None):
    device = lax.axis_index("ctx") if device is None else device
    odd = jnp.bitwise_and(device, 1) ^ other
    return 2 * slot if slot not in (1, 2) else jnp.where(odd == 1, 2 * (3 - slot), 2 * slot)


def part(index, size):
    return pl.ds(index * size if isinstance(index, int) else pl.multiple_of(index * size, size), size)


def cross_spectrum(first, left, right, half, scale):
    lc, ls, rc, rs = left[:, :half], left[:, half:], right[:, :half], right[:, half:]
    cc, ss = lc * rc, ls * rs
    real, imag = cc + ss, ls * rc - lc * rs
    if first:
        lane = lax.broadcasted_iota(jnp.int32, lc.shape, 1) == 0
        real = jnp.where(lane, 0.5 * cc, real)
        imag = jnp.where(lane, 0.5 * ss, imag)
    return jnp.concatenate([(scale * real).astype(BF16), (scale * imag).astype(BF16)], axis=1)


def blocks(table_ref):
    length, period = table_ref.shape
    width = 2 * min(HALF, length)
    return [slice(i, i + width) for i in range(0, period, width)]


def pack_kernel(chips, tok_ref, sibling_ref, *refs):
    pack_refs = refs[-chips:]
    chans = pack_refs[0].shape[1]
    for i, pack_ref in enumerate(pack_refs):
        rows = part(own_index(chip_offset(i)), chans)
        pack_ref[0] = tok_ref[rows, :]
        pack_ref[1] = sibling_ref[rows, :]


def unpack(pack_refs, signal):
    tokens = pack_refs[0].shape[2]
    for i, pack_ref in enumerate(pack_refs):
        for j in range(2):
            signal[:, part(own_index(chip_offset(i) ^ j), tokens)] = pack_ref[j]


def filter_spec_kernel(filt_ref, table_ref, spec_ref):
    spec_ref[...] = dot(filt_ref[...].astype(BF16), table_ref[...])


def rank_acts_kernel(down_ref, tok_ref, out_ref):
    out_ref[...] = dot(down_ref[...], tok_ref[...]).astype(BF16)


def grad_u_kernel(groups, filt_spec_ref, up_ref, acts_ref, table_ref, *refs):
    pack_refs, (spec_ref, keep_ref, give_ref, rank_out, signal, cross, du, rank_ref, sems) = refs[:-9], refs[-9:]
    length = table_ref.shape[0]
    chips = len(pack_refs)
    _, chans, tokens = pack_refs[0].shape
    unpack(pack_refs, signal)
    for cols in blocks(table_ref):
        half = (cols.stop - cols.start) // 2
        spec = dot(signal[...], table_ref[:, cols])
        spec_ref[:, cols] = spec.astype(BF16)
        cross[:, cols] = cross_spectrum(cols.start == 0, spec, filt_spec_ref[:, cols], half, 1.0 / length)
    grad_u = dot_nt(cross[...], table_ref[...]).astype(BF16)
    du[...] = grad_u
    rank = dot(up_ref[:, part(own_index(0), chans)], grad_u).astype(BF16)
    for i in range(2 * chips):
        for j in range(groups):
            rank_ref[i * groups + j, : rank.shape[0]] = rank[:, i * tokens : (i + 1) * tokens]
            rank_ref[i * groups + j, rank.shape[0] :] = acts_ref[...]
    copy = pltpu.make_async_copy(rank_ref, rank_out, sems.at[0])
    copy.start()
    for i in range(chips):
        for j, out_ref in enumerate((keep_ref, give_ref)):
            out_ref[i] = du[:, part(own_index(chip_offset(i, j) ^ j), tokens)]
    copy.wait()


def pairwise(values):
    while len(values) > 1:
        values = [values[i] + values[i + 1] for i in range(0, len(values), 2)]
    return values[0]


def du_pack_kernel(keep_ref, got_ref, *pack_refs):
    for i, pack_ref in enumerate(pack_refs):
        pack_ref[0] = keep_ref[i + 1]
        pack_ref[1] = got_ref[i + 1]


def rank_kernel(groups, scale, parts_ref, tok_ref, keep_ref, give_ref, rank_ref, acts_ref, adapter_ref):
    ranks, tokens = rank_ref.shape
    width = tok_ref.shape[0]
    shards = parts_ref.shape[0] // groups
    total = None
    for i in range(shards):
        both = parts_ref[i * groups].astype(F32)
        for j in range(1, groups):
            both = both + parts_ref[i * groups + j].astype(F32)
        acts_ref[:, i * tokens : (i + 1) * tokens] = both[ranks:].astype(BF16)
        total = both[:ranks] if total is None else total + both[:ranks]
    rank_grad = total.astype(BF16)
    rank_ref[...] = rank_grad
    adapter_ref[:, :width] = scale * dot_nt(rank_grad, tok_ref[...])
    up = None
    for i in range(shards // 2):
        for j, ref in enumerate((keep_ref, give_ref)):
            term = dot_nt(acts_ref[:, part(own_index(chip_offset(i, j) ^ j), tokens)], ref[i])
            up = term if up is None else up + term
    adapter_ref[:, width:] = scale * up


def chip_sum_kernel(own_ref, other_ref, out_ref):
    chans = out_ref.shape[1] - own_ref.shape[1]
    width = own_ref.shape[1] - chans
    out_ref[:, :width] = (own_ref[:, :width] + other_ref[:, :width]).astype(BF16)
    out_ref[:, width : width + chans] = own_ref[:, width:].astype(BF16)
    out_ref[:, width + chans :] = other_ref[:, width:].astype(BF16)


def filter_grad_kernel(acts_ref, up_ref, spec_ref, table_ref, *refs):
    pack_refs, (out_ref, signal, cross, out, sems) = refs[:-5], refs[-5:]
    length = table_ref.shape[0]
    chans = pack_refs[0].shape[1]
    unpack(pack_refs, signal)
    own_up = up_ref[:, part(own_index(0), chans)]
    act = (signal[...].astype(F32) + dot_tn(own_up, acts_ref[...])).astype(BF16)
    for cols in blocks(table_ref):
        half = (cols.stop - cols.start) // 2
        spec = dot(act, table_ref[:, cols])
        cross[:, cols] = cross_spectrum(cols.start == 0, spec_ref[:, cols].astype(F32), spec, half, 1.0 / length)
    copies = []
    for i in range(sems.shape[0]):
        lags = part(i, length // sems.shape[0])
        out[:, lags] = dot_nt(cross[...], table_ref[lags, :])
        copies.append(pltpu.make_async_copy(out.at[:, lags], out_ref.at[:, lags], sems.at[i]))
        copies[-1].start()
    for copy in copies:
        copy.wait()


def input_grad_kernel(keep_ref, got_ref, down_ref, rank_ref, *refs):
    pack_refs, out_ref = refs[:-1], refs[-1]
    chans = keep_ref.shape[1]

    def put(offset, value):
        index = own_index(offset)
        lift = dot_tn(down_ref[:, part(index, chans)], rank_ref[...])
        out_ref[part(index, chans), :] = (value.astype(F32) + lift).astype(BF16)

    put(0, keep_ref[0])
    put(1, got_ref[0])
    for i, pack_ref in enumerate(pack_refs):
        for j in range(2):
            put(chip_offset(i + 1) ^ j, pack_ref[j])


def adapter_sum_kernel(*refs):
    part_refs, down_out, up_out, total, chunks = refs[:-4], refs[-4], refs[-3], refs[-2], refs[-1]
    width = down_out.shape[2]
    chans = (part_refs[0].shape[1] - width) // 2
    sums = [ref[:, :width].astype(F32) for ref in part_refs]
    down_out[:, 0, :] = pairwise(sums)
    for i, ref in enumerate(part_refs):
        for j in range(2):
            block = ref[:, width + j * chans : width + (j + 1) * chans]
            chunks[:, part(own_index(2 * i + j), chans)] = block.astype(F32)
    up_out[:, 0, :] = chunks[...]


def dense_body(mesh, saved_input, out_grad, filters, adapter_down, adapter_up):
    shards, groups = mesh.shape["ctx"], mesh.shape["grp"]
    tok_input, tok_grad, filt = saved_input[0], out_grad[0], filters[0]
    down, up = adapter_down[:, 0, :], adapter_up[:, 0, :]
    rank, width = down.shape
    tokens = tok_input.shape[1]
    chans, length = filt.shape
    chips = shards // 2
    table = jnp.asarray(dft_table(length))
    local = pl.BlockSpec(memory_space=pltpu.VMEM)
    product = 2 * chans * length * 2 * length

    def call(kernel, name, out_shape, args, scratch=(), flops=0, early=0, far_out=()):
        outs = jax.tree.leaves(out_shape)
        moved = sum(int(np.prod(o.shape)) * o.dtype.itemsize for o in outs)
        out_specs = tuple(pl.BlockSpec(memory_space=pl.ANY) if i in far_out else local for i in range(len(outs)))
        out_specs = out_specs if isinstance(out_shape, tuple) else out_specs[0]
        return pl.pallas_call(
            kernel,
            out_shape=out_shape,
            in_specs=[local] * (len(args) - early) + [pl.BlockSpec(memory_space=pl.ANY)] * early,
            out_specs=out_specs,
            scratch_shapes=scratch,
            cost_estimate=pl.CostEstimate(flops=flops, bytes_accessed=moved, transcendentals=0),
            compiler_params=pltpu.CompilerParams(vmem_limit_bytes=VMEM_BYTES),
            name=name,
        )(*args)

    def send(value, offset, axis="ctx"):
        return lax.ppermute(value, axis, [(i, i ^ offset) for i in range(mesh.shape[axis])])

    def packed(own, sibling, name, early=(), flops=0):
        kernel = functools.partial(pack_kernel, chips)
        return call(kernel, name, (pack,) * chips, (own, sibling, *early), early=len(early), flops=flops)

    def to_chip(value, slot):
        other = slot if chips < 4 or slot not in (1, 2) else 3 - slot
        pairs = [(i, i ^ (2 * (other if i % 2 else slot))) for i in range(shards)]
        return lax.ppermute(value, "ctx", pairs)

    def to_chips(packs):
        return [packs[0]] + [to_chip(packs[i], i) for i in range(1, chips)]

    vmem = pltpu.VMEM
    pack = shape((2, chans, tokens), BF16)
    sibling_grad = send(tok_grad, 1)
    sibling_input = send(tok_input, 1)
    ahead = 4 * product
    first = call(lambda out_ref: out_ref.__setitem__(Ellipsis, jnp.zeros_like(out_ref)), "first", shape((8, 128), F32), (), flops=ahead)
    grad_packs = packed(tok_grad, sibling_grad, "grad_pack", (first,), ahead)
    chan_grad = to_chips(grad_packs)
    everyone = shards * groups
    acts_part = call(rank_acts_kernel, "rank_acts", shape((rank, tokens), BF16), (down, tok_input))
    filt_spec = call(filter_spec_kernel, "filter_spec", shape((chans, 2 * length), F32), (filt, table), flops=product)
    half_du = shape((chips, chans, tokens), BF16)
    grad_spec, keep, give, rank_parts = call(
        functools.partial(grad_u_kernel, groups),
        "grad_u",
        (shape((chans, 2 * length), BF16), half_du, half_du, shape((everyone, 2 * rank, tokens), BF16)),
        (filt_spec, up, acts_part, table, *chan_grad),
        scratch=[
            vmem((chans, length), BF16),
            vmem((chans, 2 * length), BF16),
            vmem((chans, length), BF16),
            vmem((everyone, 2 * rank, tokens), BF16),
            pltpu.SemaphoreType.DMA((1,)),
        ],
        far_out=(3,),
    )
    chan_packs = to_chips(packed(tok_input, sibling_input, "input_pack"))
    late_pack = chan_packs.pop(1)
    rank_parts, chan_packs = lax.optimization_barrier((rank_parts, chan_packs))
    all_parts = lax.all_to_all(rank_parts, ("ctx", "grp"), 0, 0, tiled=True)
    got = send(give, 1)
    du_packs = call(du_pack_kernel, "du_pack", (pack,) * (chips - 1), (keep, got))
    tok_packs = [to_chip(du_packs[i], i + 1) for i in range(chips - 1)]
    all_parts, tok_packs[:2], late_pack = lax.optimization_barrier((all_parts, tok_packs[:2], late_pack))
    chan_packs.insert(1, late_pack)
    rank_grad, acts, adapter_part = call(
        functools.partial(rank_kernel, groups, float(length) ** -0.5),
        "rank_grad",
        (shape((rank, tokens), BF16), shape((rank, length), BF16), shape((rank, width + chans), F32)),
        (all_parts, tok_input, keep, give),
        flops=ahead,
    )
    other_part = send(adapter_part, 1)
    chip_part = call(
        chip_sum_kernel,
        "chip_sum",
        shape((rank, width + 2 * chans), BF16),
        (adapter_part, other_part),
    )
    chip_parts = [chip_part] + [send(chip_part, 2 * i) for i in range(1, chips)]
    filt_grad = call(
        filter_grad_kernel,
        "filter_grad",
        shape((chans, length), F32),
        (acts, up, grad_spec, table, *chan_packs),
        scratch=[
            vmem((chans, length), BF16),
            vmem((chans, 2 * length), BF16),
            vmem((chans, length), F32),
            pltpu.SemaphoreType.DMA((2,)),
        ],
        flops=2 * product,
        far_out=(0,),
    )
    filt_grad, got = lax.optimization_barrier((filt_grad, got))
    grad_input = call(
        input_grad_kernel, "input_grad", shape((width, tokens), BF16), (keep, got, down, rank_grad, *tok_packs)
    )
    grad_down, grad_up = call(
        adapter_sum_kernel,
        "adapter_sum",
        (shape((rank, 1, width), F32),) * 2,
        chip_parts,
        scratch=[pltpu.VMEM((rank, width), F32)] * 2,
    )
    return grad_input[None], filt_grad[None], grad_down, grad_up


def split_radix(points):
    radix_low = 1
    while (
        points % (radix_low * 2) == 0
        and radix_low * 2 * (radix_low * 2) <= points
        and (points // (radix_low * 2) % 2 == 0)
    ):
        radix_low = radix_low * 2
    return (radix_low, points // radix_low)


def angle_table(height, across, period):
    index_down = lax.broadcasted_iota(jnp.int32, (height, across), 0)
    index_across = lax.broadcasted_iota(jnp.int32, (height, across), 1)
    phase = (index_down * index_across % period).astype(jnp.float32) * (2.0 * math.pi / period)
    return (jnp.cos(phase), jnp.sin(phase))


def make_tables(points):
    radix_low, radix_high = split_radix(points)
    cos_one, sin_one = angle_table(radix_high, radix_high // 2, radix_high)
    first = jnp.concatenate([cos_one, -sin_one], axis=0)
    first_high = first.astype(jnp.bfloat16)
    first_low = (first - first_high.astype(jnp.float32)).astype(jnp.bfloat16)
    twist = angle_table(radix_high, radix_low, points)
    cos_two, sin_two = angle_table(radix_low, radix_low, radix_low)
    second_fwd = jnp.concatenate(
        [jnp.concatenate([cos_two, sin_two], axis=1), jnp.concatenate([-sin_two, cos_two], axis=1)],
        axis=0,
    )
    second_inv = jnp.concatenate(
        [jnp.concatenate([cos_two, -sin_two], axis=1), jnp.concatenate([sin_two, cos_two], axis=1)],
        axis=0,
    )
    last_inv = jnp.concatenate([cos_one, -sin_one], axis=0)
    return (
        radix_low,
        radix_high,
        first,
        first_high,
        first_low,
        twist,
        second_fwd,
        second_inv,
        last_inv,
    )


def forward_dft(signal, tables):
    radix_low, radix_high, first, first_high, first_low, twist, second_fwd, second_inv, last_inv = (
        tables
    )
    channels = signal.shape[0]
    blocks = signal.reshape(channels, radix_high // 2, radix_low)
    if signal.dtype == jnp.bfloat16:
        section_one = jnp.einsum(
            "kn,cnp->ckp", first_high, blocks, preferred_element_type=jnp.float32
        )
        section_one = section_one + jnp.einsum(
            "kn,cnp->ckp", first_low, blocks, preferred_element_type=jnp.float32
        )
    else:
        section_one = jnp.einsum("kn,cnp->ckp", first, blocks, precision=HIGH)
    real_one = section_one[:, :radix_high]
    imag_one = section_one[:, radix_high:]
    cos_twist, sin_twist = twist
    real_two = real_one * cos_twist + imag_one * sin_twist
    imag_two = imag_one * cos_twist - real_one * sin_twist
    joined = jnp.concatenate([real_two, imag_two], axis=2)
    spectrum = jnp.einsum("jq,ckq->cjk", second_fwd, joined, precision=HIGH)
    return (spectrum[:, :radix_low], spectrum[:, radix_low:])


def inverse_dft(spectrum, tables):
    radix_low, radix_high, first, first_high, first_low, twist, second_fwd, second_inv, last_inv = (
        tables
    )
    spec_real, spec_imag = spectrum
    channels = spec_real.shape[0]
    joined = jnp.concatenate([spec_real, spec_imag], axis=1)
    section_one = jnp.einsum("pq,cqk->cpk", second_inv, joined, precision=HIGH)
    real_one = section_one[:, :radix_low]
    imag_one = section_one[:, radix_low:]
    cos_twist = twist[0].T
    sin_twist = twist[1].T
    real_two = real_one * cos_twist - imag_one * sin_twist
    imag_two = real_one * sin_twist + imag_one * cos_twist
    stacked = jnp.concatenate([real_two, imag_two], axis=2)
    signal = jnp.einsum("kn,cpk->cnp", last_inv, stacked, precision=HIGH)
    return signal.reshape(channels, -1) / float(radix_low * radix_high)


def conj_product(spec_left, spec_right):
    left_real, left_imag = spec_left
    right_real, right_imag = spec_right
    return (
        left_real * right_real + left_imag * right_imag,
        left_imag * right_real - left_real * right_imag,
    )


def staged_body(saved_input, out_grad, filters, adapter_down, adapter_up):
    tok_input = saved_input[0]
    tok_grad = out_grad[0]
    down_rows = adapter_down[:, 0, :]
    up_float = adapter_up[:, 0, :].astype(jnp.float32)
    rank_part = jnp.dot(down_rows, tok_input, preferred_element_type=jnp.float32)
    rank_acts = lax.psum(rank_part, "grp")
    tok_act = (
        tok_input.astype(jnp.float32) + jnp.einsum("rc,rt->ct", up_float, rank_acts, precision=HIGH)
    ).astype(jnp.bfloat16)
    chan_act, chan_grad = (
        lax.all_to_all(tok_act, "ctx", split_axis=0, concat_axis=1, tiled=True),
        lax.all_to_all(tok_grad, "ctx", split_axis=0, concat_axis=1, tiled=True),
    )
    length = chan_act.shape[1]
    tables = make_tables(2 * length)
    act_spec = forward_dft(chan_act, tables)
    grad_spec = forward_dft(chan_grad, tables)
    kern_spec = forward_dft(filters[0], tables)
    chan_du = inverse_dft(conj_product(grad_spec, kern_spec), tables).astype(jnp.bfloat16)
    filt_grad = inverse_dft(conj_product(grad_spec, act_spec), tables)
    tok_du = lax.all_to_all(chan_du, "ctx", split_axis=1, concat_axis=0, tiled=True)
    du_float = tok_du.astype(jnp.float32)
    rank_grad = lax.psum(jnp.einsum("rc,ct->rt", up_float, du_float, precision=HIGH), "grp")
    grad_input = (
        du_float + jnp.einsum("rc,rt->ct", down_rows.astype(jnp.float32), rank_grad, precision=HIGH)
    ).astype(jnp.bfloat16)
    down_part = jnp.einsum("rt,ct->rc", rank_grad, tok_input.astype(jnp.float32), precision=HIGH)
    up_part = jnp.einsum("rt,ct->rc", rank_acts, du_float, precision=HIGH)
    down_sum, up_sum = lax.psum((down_part, up_part), "ctx")
    factor = float(length) ** (-0.5)
    return (
        grad_input[None],
        filt_grad[None],
        (factor * down_sum)[:, None, :],
        (factor * up_sum)[:, None, :],
    )


def body(mesh, saved_input, out_grad, filters, adapter_down, adapter_up):
    length = filters.shape[2]
    shards, groups = mesh.shape["ctx"], mesh.shape["grp"]
    paired = shards > 1 and shards & (shards - 1) == 0 and groups & (groups - 1) == 0
    if 2 * length * length <= TABLE_ENTRIES and paired:
        return dense_body(mesh, saved_input, out_grad, filters, adapter_down, adapter_up)
    return staged_body(saved_input, out_grad, filters, adapter_down, adapter_up)


def solution(mesh):
    placed = (
        P("grp", None, "ctx"),
        P("grp", None, "ctx"),
        P("grp", "ctx", None),
        P(None, "grp", None),
        P(None, "grp", None),
    )
    return jax.shard_map(
        functools.partial(body, mesh),
        mesh=mesh,
        in_specs=placed,
        out_specs=(
            P("grp", None, "ctx"),
            P("grp", "ctx", None),
            P(None, "grp", None),
            P(None, "grp", None),
        ),
        check_vma=False,
    )
```
